128 devices in a mesh: ctx: 16 (over x_hi, z, core), head: 8 (over x_lo, y).
Axes of the slice: x: 4 (x_hi: 2, x_lo: 2; x = x_hi * 2 + x_lo), y: 4, z: 4, core: 2. Of those that a mesh axis runs over, the one named last changes fastest.
Arguments:
- hidden_in: bfloat16 [6144, 4096], P('ctx', 'head'), may hold values from -6 to 6
- query: bfloat16 [6144, 4096], P('ctx', 'head'), may hold values from -5 to 5
- key: bfloat16 [6144, 1024], P('ctx', 'head'), may hold values from -5 to 5
- value: bfloat16 [6144, 1024], P('ctx', 'head'), may hold values from -6 to 6
- out_weight: bfloat16 [4096, 4096], P('head'), may hold values from -0.09375 to 0.09375
- grad_out: bfloat16 [6144, 4096], P('ctx', 'head'), may hold values from -3 to 3
- span_map: int32 [16, 2], replicated, may hold values from 0 to 31, as said below
- owner_map: int32 [3, 16], replicated, may hold values from 0 to 15, as said below
Outputs:
- key_weight_gradient: float32 [4096, 1024], P('ctx', 'head')
- value_weight_gradient: float32 [4096, 1024], P('ctx', 'head')
- out_weight_grad: float32 [4096, 4096], P('head', 'ctx')
The draws below stay inside these ranges and needn't reach their ends.
Inputs may be any that keep to these rules, and one draw needn't show every extreme that they name: `span_map`: row i names a span c of the first 16 spans and then the span 32 - 1 - c; the first column is a permutation of 0 to 15. `owner_map`: each row is a permutation of 0 to 16 - 1.
All inputs are finite; a program needn't handle non-finite values.
Results may differ from the reference program's by a relative error of at most 0.0095.
Values may be sent and summed in bfloat16 or wider, within the bound.
No kernel may reach another device: no remote copies, remote signals or barrier semaphores. Data moves between devices by JAX's collectives and lax.ppermute only.
A program may use at most 128 MiB of HBM per device.

```python
import jax
import jax.numpy as jnp
from jax import lax

MODEL_WIDTH = 4096
QUERY_HEAD_COUNT = 32
KEY_VALUE_HEADS = 8
HEAD_SIZE = 128
SPAN = 192
SEQUENCE_TOKENS = 6144
SLOTS = 32
N_CTX = 16


def draw_query(key, part):
    key = jax.random.fold_in(key, 31)
    sampled_rows = jnp.clip(jax.random.normal(key, (SEQUENCE_TOKENS, QUERY_HEAD_COUNT * HEAD_SIZE), jnp.float32), -4.0, 4.0)
    return sampled_rows.astype(jnp.bfloat16)


def draw_key(key, part):
    key = jax.random.fold_in(key, 37)
    sampled_rows = jnp.clip(jax.random.normal(key, (SEQUENCE_TOKENS, KEY_VALUE_HEADS * HEAD_SIZE), jnp.float32), -4.0, 4.0)
    return sampled_rows.astype(jnp.bfloat16)


def draw_span_map(key, part):
    key = jax.random.fold_in(key, 11)
    order = jax.random.permutation(key, SLOTS // 2).astype(jnp.int32)
    return jnp.stack([order, SLOTS - 1 - order], axis=1).astype(jnp.int32)


def draw_owner_map(key, part):
    key = jax.random.fold_in(key, 23)
    split_keys = jax.random.split(key, 3)
    return jnp.stack([jax.random.permutation(split_keys[0], SLOTS // 2), jax.random.permutation(split_keys[1], SLOTS // 2), jax.random.permutation(split_keys[2], SLOTS // 2)]).astype(jnp.int32)


def spiked(drawn, key, source, target, parts, factor):
    owner, partner = [(jnp.arange(drawn.shape[dim]) // (drawn.shape[dim] // parts)).reshape([-1 if axis == dim else 1 for axis in range(drawn.ndim)]) for dim in (source, target)]
    chosen = jax.random.permutation(key, parts)[partner]
    strong = (owner == chosen) | (owner == (partner + parts // 2) % parts)
    return jnp.where(strong, factor * drawn, drawn)


def level_of(rng, extent, cuts, least, top_value):
    loudness = 1.0
    for axis_at, blocks in cuts:
        heights = jax.random.uniform(jax.random.fold_in(jax.random.fold_in(rng, 6), axis_at), (blocks,), jnp.float32, least / len(cuts), top_value / len(cuts))
        loudness = loudness * jnp.repeat(jnp.exp(heights), extent[axis_at] // blocks).reshape((-1,) + (1,) * (len(extent) - 1 - axis_at))
    return loudness


def normal_values(own_key, extent, scale, most, pieces=(), kind=jnp.bfloat16):
    array = scale * jax.random.normal(own_key, extent, jnp.float32)
    if pieces:
        array = array * level_of(own_key, extent, pieces, -0.22, 0.18)
    return jnp.clip(array, -most, most).astype(kind)


def heavy_noise(rng, dims, width, bound, shards, heavy, held_as=jnp.bfloat16):
    entries = width * jax.random.normal(rng, dims, jnp.float32)
    if shards:
        entries = entries * level_of(rng, dims, shards, -0.22, 0.18)
    return jnp.clip(spiked(entries, jax.random.fold_in(rng, 3), *heavy), -bound, bound).astype(held_as)


def setup_inputs(seed: int = 0) -> dict:
    key_of = jax.random.split(jax.random.key(seed), 9)
    hidden_in = heavy_noise(key_of[0], (SEQUENCE_TOKENS, MODEL_WIDTH), 1.0, 6.0, ((0, 16), (1, 8)), (0, 1, 16, 2.0))
    query = draw_query(jax.random.fold_in(key_of[8], 71), 0)
    key = draw_key(jax.random.fold_in(key_of[8], 71), 0)
    value = normal_values(key_of[3], (SEQUENCE_TOKENS, KEY_VALUE_HEADS * HEAD_SIZE), 1.0, 6.0, ((0, 16), (1, 8)))
    out_weight = normal_values(key_of[4], (QUERY_HEAD_COUNT * HEAD_SIZE, MODEL_WIDTH), MODEL_WIDTH ** -0.5, 0.09375, ((0, 8),))
    grad_out = heavy_noise(key_of[5], (SEQUENCE_TOKENS, MODEL_WIDTH), 0.5, 3.0, ((0, 16), (1, 8)), (0, 1, 16, 2.0))
    span_map = draw_span_map(jax.random.fold_in(key_of[8], 71), 0)
    owner_map = draw_owner_map(jax.random.fold_in(key_of[8], 71), 0)
    return dict(hidden_in=hidden_in, query=query, key=key, value=value, out_weight=out_weight, grad_out=grad_out, span_map=span_map, owner_map=owner_map)


def owner_order(owner_map, cycle_size):
    blocks = jnp.arange(cycle_size, dtype=jnp.int32)
    owner_match = owner_map[:, None, :] == blocks[None, :, None]
    return jnp.sum(jnp.where(owner_match, blocks[None, None, :], 0), axis=2).astype(jnp.int32)


def reference(hidden_in, query, key, value, out_weight, grad_out, span_map, owner_map):
    all_rows = jnp.arange(SEQUENCE_TOKENS, dtype=jnp.int32)
    span_ids = span_map.reshape(-1)[all_rows // SPAN]
    position = span_ids * SPAN + all_rows % SPAN
    visible = position[None, :] <= position[:, None]
    d_attn = jnp.dot(grad_out, out_weight.T, preferred_element_type=jnp.float32).astype(jnp.bfloat16)
    group_extent = QUERY_HEAD_COUNT // KEY_VALUE_HEADS
    score_scale = HEAD_SIZE ** -0.5

    def one_head(head_index):
        kv_head = head_index // group_extent
        query_head = lax.dynamic_slice_in_dim(query, (head_index * HEAD_SIZE).astype(jnp.int32), HEAD_SIZE, 1)
        d_head = lax.dynamic_slice_in_dim(d_attn, (head_index * HEAD_SIZE).astype(jnp.int32), HEAD_SIZE, 1)
        key_head = lax.dynamic_slice_in_dim(key, (kv_head * HEAD_SIZE).astype(jnp.int32), HEAD_SIZE, 1)
        value_head = lax.dynamic_slice_in_dim(value, (kv_head * HEAD_SIZE).astype(jnp.int32), HEAD_SIZE, 1)
        scores = score_scale * jnp.dot(query_head, key_head.T, preferred_element_type=jnp.float32)
        masked_scores = jnp.where(visible, scores, -1e30)
        row_top = jnp.max(masked_scores, axis=1, keepdims=True)
        row_total = jnp.sum(jnp.where(visible, jnp.exp(masked_scores - row_top), 0.0), axis=1, keepdims=True)
        row_lse = row_top + jnp.log(row_total)
        prob_rows = jnp.where(visible, jnp.exp(masked_scores - row_lse), 0.0)
        prob_low = prob_rows.astype(jnp.bfloat16)
        attn_head = jnp.dot(prob_low, value_head, preferred_element_type=jnp.float32).astype(jnp.bfloat16)
        row_delta = jnp.sum(d_head.astype(jnp.float32) * attn_head.astype(jnp.float32), axis=1, keepdims=True)
        d_probs = jnp.dot(d_head, value_head.T, preferred_element_type=jnp.float32)
        d_scores = (prob_rows * (d_probs - row_delta)).astype(jnp.bfloat16)
        d_key_head = score_scale * jnp.dot(d_scores.T, query_head, preferred_element_type=jnp.float32)
        d_value_head = jnp.dot(prob_low.T, d_head, preferred_element_type=jnp.float32)
        return attn_head, d_key_head, d_value_head

    attn_heads, key_head_gradients, value_head_gradients = lax.map(one_head, jnp.arange(QUERY_HEAD_COUNT, dtype=jnp.int32))
    attn = jnp.transpose(attn_heads, (1, 0, 2)).reshape(SEQUENCE_TOKENS, QUERY_HEAD_COUNT * HEAD_SIZE)
    key_gradient_total = jnp.sum(key_head_gradients.reshape(KEY_VALUE_HEADS, group_extent, SEQUENCE_TOKENS, HEAD_SIZE), axis=1)
    value_gradient_total = jnp.sum(value_head_gradients.reshape(KEY_VALUE_HEADS, group_extent, SEQUENCE_TOKENS, HEAD_SIZE), axis=1)
    key_gradient = jnp.transpose(key_gradient_total, (1, 0, 2)).reshape(SEQUENCE_TOKENS, KEY_VALUE_HEADS * HEAD_SIZE)
    value_gradient = jnp.transpose(value_gradient_total, (1, 0, 2)).reshape(SEQUENCE_TOKENS, KEY_VALUE_HEADS * HEAD_SIZE)
    hidden_wide = hidden_in.astype(jnp.float32)
    key_projection_gradient = jnp.dot(hidden_wide.T, key_gradient, preferred_element_type=jnp.float32, precision=lax.Precision.HIGHEST)
    value_projection_gradient = jnp.dot(hidden_wide.T, value_gradient, preferred_element_type=jnp.float32, precision=lax.Precision.HIGHEST)
    out_grad = jnp.dot(attn.T, grad_out, preferred_element_type=jnp.float32)
    inverse_permutation = owner_order(owner_map, N_CTX)
    block_extent = MODEL_WIDTH // N_CTX
    key_weight_gradient = key_projection_gradient.reshape(N_CTX, block_extent, KEY_VALUE_HEADS * HEAD_SIZE)[inverse_permutation[0]].reshape(MODEL_WIDTH, KEY_VALUE_HEADS * HEAD_SIZE)
    value_weight_gradient = value_projection_gradient.reshape(N_CTX, block_extent, KEY_VALUE_HEADS * HEAD_SIZE)[inverse_permutation[1]].reshape(MODEL_WIDTH, KEY_VALUE_HEADS * HEAD_SIZE)
    out_weight_grad = out_grad.reshape(QUERY_HEAD_COUNT * HEAD_SIZE, N_CTX, block_extent)[:, inverse_permutation[2]].reshape(QUERY_HEAD_COUNT * HEAD_SIZE, MODEL_WIDTH)
    return key_weight_gradient, value_weight_gradient, out_weight_grad
```

```python
import functools

import jax
import jax.numpy as jnp
from jax import lax
from jax.experimental import pallas as pl
from jax.experimental.pallas import tpu as pltpu
from jax.sharding import PartitionSpec as P

MODEL_WIDTH = 4096
HEAD_SIZE = 128
GROUP = 4
SPAN = 192
SLOTS = 32
N_CTX = 16
CHIPS = 8
TOKENS = 384
KEY_BLOCK = 384
KEY_BLOCKS = 16
LANES = GROUP * SPAN
CHUNK = 256
SCALE = HEAD_SIZE ** (-0.5)
EXP2_SCALE = SCALE * 1.4426950408889634
F32 = jnp.float32
BF16 = jnp.bfloat16
VMEM_BYTES = 58 * 1024 * 1024


def ctx_move(value, dx, dz, dc):
    pairs = []
    for i in range(N_CTX):
        x, z, c = i // 8, (i // 2) % 4, i % 2
        pairs.append((i, ((x ^ dx) * 4 + (z + dz) % 4) * 2 + (c ^ dc)))
    return lax.ppermute(value, "ctx", pairs)


def head_move(value, dx, dy):
    pairs = [(i, ((i // 4) ^ dx) * 4 + (i % 4 + dy) % 4) for i in range(8)]
    return lax.ppermute(value, "head", pairs)


def gather_over_head(own):
    across = head_move(own, 1, 0)
    up0 = head_move(own, 0, 1)
    down0 = head_move(own, 0, 3)
    up1 = head_move(across, 0, 1)
    down1 = head_move(across, 0, 3)
    far0 = head_move(up0, 0, 1)
    far1 = head_move(down1, 0, 3)
    return [own, across, up0, down0, up1, down1, far0, far1]


HEAD_STEPS = ((0, 0), (1, 0), (0, 3), (0, 1), (1, 3), (1, 1), (0, 2), (1, 2))


def gather_over_ctx(own):
    pair = jnp.concatenate([own, ctx_move(own, 1, 0, 0)], axis=0)
    mine = [pair] + [ctx_move(pair, 0, step, 0) for step in (1, 3, 2)]
    return mine + [ctx_move(piece, 0, 0, 1) for piece in mine]


CTX_STEPS = tuple((dz, dc) for dc in (0, 1) for dz in (0, 3, 1, 2))


def nt(a, b):
    return lax.dot_general(a, b, (((1,), (1,)), ((), ())), preferred_element_type=F32)


def nn(a, b):
    return lax.dot_general(a, b, (((1,), (0,)), ((), ())), preferred_element_type=F32)


def attention_kernel(ids, spans, q_ref, do_ref, *rest):
    kv_refs, rest = rest[:8], rest[8:]
    attn_ref, own_ref, other_ref, ks, vs, vt, qs, dos, st, tops, slot, acc_k, acc_v = rest
    ctx = ids[0]
    my_x, my_z, my_c = ctx // 8, (ctx // 2) % 4, ctx % 2
    low = spans[ctx, 0]

    for i in range(N_CTX):
        for half in range(2):
            slot[spans[i, half]] = (my_c ^ (i % 2)) * 16 + (i // 2) * 2 + half

    for piece, (dz, dc) in enumerate(CTX_STEPS):
        for dx in range(2):
            source = ((my_x ^ dx) * 4 + (my_z + dz) % 4) * 2 + (my_c ^ dc)
            for half in range(2):
                span = spans[source, half]
                at = pl.ds(pl.multiple_of(span * SPAN, SPAN), SPAN)
                rows = pl.ds((dx * 2 + half) * SPAN, SPAN)
                ks[at, :] = kv_refs[piece][rows, :HEAD_SIZE]
                vs[at, :] = kv_refs[piece][rows, HEAD_SIZE:]
    for half in range(2):
        for h in range(GROUP):
            rows, cols = pl.ds(half * SPAN, SPAN), pl.ds(h * HEAD_SIZE, HEAD_SIZE)
            qs[half, pl.ds(h * SPAN, SPAN), :] = q_ref[rows, cols]
            dos[half, pl.ds(h * SPAN, SPAN), :] = do_ref[rows, cols]

    def key_rows(b):
        return pl.ds(pl.multiple_of(b * KEY_BLOCK, KEY_BLOCK), KEY_BLOCK)

    @pl.loop(0, KEY_BLOCKS)
    def _(b):
        vt[b] = vs[key_rows(b), :].astype(F32).T.astype(BF16)

    lane = lax.broadcasted_iota(jnp.int32, (1, LANES), 1)
    within = lane
    for h in range(1, GROUP):
        within = within - jnp.where(lane >= h * SPAN, SPAN, 0)
    chunks = [pl.ds(at, CHUNK) for at in range(0, LANES, CHUNK)]
    span_of = (low, SLOTS - 1 - low)
    last = (span_of[0] // 2, span_of[1] // 2)

    def tile_index(half, b):
        return b if half == 1 else KEY_BLOCKS - b

    inverse, delta = [], []
    for half in (1, 0):

        def score(b, masked):
            key_block = ks[key_rows(b), :]
            for n, chunk in enumerate(chunks):
                scores = nt(key_block, qs[half, chunk, :])
                if masked:
                    keys = lax.broadcasted_iota(jnp.int32, (KEY_BLOCK, CHUNK), 0) + b * KEY_BLOCK
                    at = span_of[half] * SPAN + within[:, n * CHUNK : (n + 1) * CHUNK]
                    scores = jnp.where(keys > at, -1e30, scores)
                st[tile_index(half, b), :, chunk] = scores
                tops[:, chunk] = jnp.maximum(tops[:, chunk], jnp.max(scores, axis=0, keepdims=True))

        tops[...] = jnp.full((1, LANES), -1e30, F32)

        @pl.loop(0, last[half])
        def _(b):
            score(b, False)

        score(last[half], True)
        top = tops[...]
        acc_v[...] = jnp.zeros((HEAD_SIZE, LANES), F32)
        tops[...] = jnp.zeros((1, LANES), F32)

        @pl.loop(0, last[half] + 1)
        def _(b):
            values_t = vt[b]
            for n, chunk in enumerate(chunks):
                tile = st.at[tile_index(half, b)]
                p = jnp.exp2((tile[:, chunk] - top[:, n * CHUNK : (n + 1) * CHUNK]) * EXP2_SCALE)
                tile[:, chunk] = p
                tops[:, chunk] += jnp.sum(p, axis=0, keepdims=True)
                acc_v[:, chunk] += nn(values_t, p.astype(BF16))

        inv = 1.0 / tops[...]
        attn_t = (acc_v[...] * inv).astype(BF16).astype(F32)
        do_t = dos[half].astype(F32).T
        inverse.insert(0, inv)
        delta.insert(0, jnp.sum(attn_t * do_t, axis=0, keepdims=True))
        attn = attn_t.T.astype(BF16)
        for h in range(GROUP):
            attn_ref[pl.ds(half * SPAN, SPAN), pl.ds(h * HEAD_SIZE, HEAD_SIZE)] = attn[
                h * SPAN : (h + 1) * SPAN
            ]

    def gradients(b, halves):
        value_block = vs[key_rows(b), :]
        d_key = jnp.zeros((KEY_BLOCK, HEAD_SIZE), F32)
        d_value = jnp.zeros((KEY_BLOCK, HEAD_SIZE), F32)
        for half in halves:
            for n, chunk in enumerate(chunks):
                part = slice(n * CHUNK, (n + 1) * CHUNK)
                p = st[tile_index(half, b), :, chunk] * inverse[half][:, part]
                d_p = nt(value_block, dos[half, chunk, :])
                d_s = (p * (d_p - delta[half][:, part])).astype(BF16)
                d_key += nn(d_s, qs[half, chunk, :])
                d_value += nn(p.astype(BF16), dos[half, chunk, :])
        store(b, (d_key * SCALE).astype(BF16), d_value.astype(BF16))

    def store(b, d_key, d_value):
        for n in range(2):
            at = slot[b * 2 + n]
            rows = slice(n * SPAN, (n + 1) * SPAN)

            @pl.when(at < 16)
            def _():
                own_ref[at, :, :HEAD_SIZE] = d_key[rows]
                own_ref[at, :, HEAD_SIZE:] = d_value[rows]

            @pl.when(at >= 16)
            def _():
                other_ref[at - 16, :, :HEAD_SIZE] = d_key[rows]
                other_ref[at - 16, :, HEAD_SIZE:] = d_value[rows]

    @pl.loop(0, last[0] + 1)
    def _(b):
        gradients(b, (0, 1))

    @pl.loop(last[0] + 1, last[1] + 1)
    def _(b):
        gradients(b, (1,))

    @pl.loop(last[1] + 1, KEY_BLOCKS)
    def _(b):
        zero = jnp.zeros((KEY_BLOCK, HEAD_SIZE), BF16)
        store(b, zero, zero)


def smem():
    return pl.BlockSpec(memory_space=pltpu.SMEM)


def vmem():
    return pl.BlockSpec(memory_space=pltpu.VMEM)


def attention(ids, span_map, query, d_attn, kv_pieces):
    part = jax.ShapeDtypeStruct((2 * CHIPS, SPAN, 2 * HEAD_SIZE), BF16)
    return pl.pallas_call(
        attention_kernel,
        out_shape=(jax.ShapeDtypeStruct(query.shape, BF16), part, part),
        in_specs=[smem(), smem()] + [vmem()] * 10,
        out_specs=(vmem(),) * 3,
        scratch_shapes=[
            pltpu.VMEM((KEY_BLOCKS * KEY_BLOCK, HEAD_SIZE), BF16),
            pltpu.VMEM((KEY_BLOCKS * KEY_BLOCK, HEAD_SIZE), BF16),
            pltpu.VMEM((KEY_BLOCKS, HEAD_SIZE, KEY_BLOCK), BF16),
            pltpu.VMEM((2, LANES, HEAD_SIZE), BF16),
            pltpu.VMEM((2, LANES, HEAD_SIZE), BF16),
            pltpu.VMEM((KEY_BLOCKS + 1, KEY_BLOCK, LANES), F32),
            pltpu.VMEM((1, LANES), F32),
            pltpu.SMEM((SLOTS,), jnp.int32),
            pltpu.VMEM((HEAD_SIZE, LANES), F32),
            pltpu.VMEM((HEAD_SIZE, LANES), F32),
        ],
        compiler_params=pltpu.CompilerParams(vmem_limit_bytes=VMEM_BYTES),
        cost_estimate=pl.CostEstimate(
            flops=13_000_000_000, bytes_accessed=8_000_000, transcendentals=5_000_000
        ),
        name="attention",
    )(ids, span_map, query, d_attn, *kv_pieces)


def out_grad_kernel(ids, owners, attn_ref, *rest):
    pieces, (own_ref, other_ref) = rest[:8], rest[8:]
    my_x, my_y, my_c = ids[1] // 4, ids[1] % 4, ids[0] % 2
    attn_t = attn_ref[...].astype(F32).T.astype(BF16)
    for piece, (dx, dy) in zip(pieces, HEAD_STEPS):
        source = (my_x ^ dx) * 4 + (my_y + dy) % 4
        for half in range(2):
            owner = owners[2, source * 2 + half]
            block = nn(attn_t, piece[:, pl.ds(half * 256, 256)]).astype(BF16)

            @pl.when(owner % 2 == my_c)
            def _():
                own_ref[owner // 2] = block

            @pl.when(owner % 2 != my_c)
            def _():
                other_ref[owner // 2] = block


def out_gradient(ids, owner_map, attn, pieces):
    part = jax.ShapeDtypeStruct((CHIPS, 512, 256), BF16)
    return pl.pallas_call(
        out_grad_kernel,
        out_shape=(part, part),
        in_specs=[smem(), smem()] + [vmem()] * 9,
        out_specs=(vmem(),) * 2,
        compiler_params=pltpu.CompilerParams(vmem_limit_bytes=VMEM_BYTES),
        cost_estimate=pl.CostEstimate(
            flops=1_600_000_000, bytes_accessed=8_000_000, transcendentals=0
        ),
        name="out_gradient",
    )(ids, owner_map, attn, *pieces)


def kv_grad_kernel(ids, owners, parts_ref, hidden_ref, own_ref, other_ref):
    my_c = ids[0] % 2
    total = jnp.sum(parts_ref[...].astype(F32), axis=0)
    high = total.astype(BF16)
    rest = (total - high.astype(F32)).astype(BF16)

    for source in range(8):
        for half in range(2):
            columns = hidden_ref[source, :, pl.ds(half * 256, 256)].astype(F32).T.astype(BF16)
            block = (nn(columns, high) + nn(columns, rest)).astype(BF16)
            for n in range(2):
                owner = owners[n, source * 2 + half]
                lanes = slice(n * HEAD_SIZE, (n + 1) * HEAD_SIZE)

                @pl.when(owner % 2 == my_c)
                def _():
                    own_ref[owner // 2, :, lanes] = block[:, lanes]

                @pl.when(owner % 2 != my_c)
                def _():
                    other_ref[owner // 2, :, lanes] = block[:, lanes]


def kv_gradient(ids, owner_map, parts, hidden):
    part = jax.ShapeDtypeStruct((CHIPS, 256, 2 * HEAD_SIZE), BF16)
    return pl.pallas_call(
        kv_grad_kernel,
        out_shape=(part, part),
        in_specs=[smem(), smem(), vmem(), vmem()],
        out_specs=(vmem(),) * 2,
        compiler_params=pltpu.CompilerParams(vmem_limit_bytes=VMEM_BYTES),
        cost_estimate=pl.CostEstimate(
            flops=1_600_000_000, bytes_accessed=7_000_000, transcendentals=0
        ),
        name="kv_gradient",
    )(ids, owner_map, parts, hidden)


def chip_sum(own, other):
    arrived = ctx_move(other, 0, 0, 1)
    return (own.astype(F32) + arrived.astype(F32)).astype(BF16)


SAME_CORE = [[c + 2 * chip for chip in range(CHIPS)] for c in range(2)]


def exchange(parts):
    return lax.all_to_all(parts, "ctx", 0, 0, tiled=True, axis_index_groups=SAME_CORE)


def per_device(hidden_in, query, key, value, out_weight, grad_out, span_map, owner_map):
    ids = jnp.stack([lax.axis_index("ctx"), lax.axis_index("head")]).astype(jnp.int32)
    grad_pieces = gather_over_head(grad_out)
    kv_pieces = gather_over_ctx(jnp.concatenate([key, value], axis=1))
    my_x, my_y = lax.axis_index("head") // 4, lax.axis_index("head") % 4
    d_attn = jnp.zeros(query.shape, F32)
    for piece, (dx, dy) in zip(grad_pieces, HEAD_STEPS):
        source = (my_x ^ dx) * 4 + (my_y + dy) % 4
        weight = lax.dynamic_slice_in_dim(out_weight, source * 512, 512, 1)
        d_attn = d_attn + nt(piece, weight)
    d_attn = d_attn.astype(BF16)
    hidden_late, _ = lax.optimization_barrier((hidden_in, grad_pieces[-1]))
    hidden = lax.all_gather(hidden_late, "head", axis=0, tiled=False)
    attn, dkv_own, dkv_other = attention(ids, span_map, query, d_attn, kv_pieces)
    dkv = exchange(chip_sum(dkv_own, dkv_other))
    out_own, out_other = out_gradient(ids, owner_map, attn, grad_pieces)
    out_parts = exchange(chip_sum(out_own, out_other))
    kv_own, kv_other = kv_gradient(
        ids, owner_map, dkv.reshape(CHIPS, TOKENS, 2 * HEAD_SIZE), hidden
    )
    kv_parts = exchange(chip_sum(kv_own, kv_other))
    kv_total = jnp.sum(kv_parts.astype(F32), axis=0)
    out_total = jnp.sum(out_parts.astype(F32), axis=0)
    return kv_total[:, :HEAD_SIZE], kv_total[:, HEAD_SIZE:], out_total


def solution(mesh):
    return jax.shard_map(
        per_device,
        mesh=mesh,
        in_specs=(
            P("ctx", "head"),
            P("ctx", "head"),
            P("ctx", "head"),
            P("ctx", "head"),
            P("head", None),
            P("ctx", "head"),
            P(),
            P(),
        ),
        out_specs=(P("ctx", "head"), P("ctx", "head"), P("head", "ctx")),
        check_vma=False,
    )
```

```python
import jax
import jax.numpy as jnp
from jax import lax
from jax.experimental import pallas as pl
from jax.experimental.pallas import tpu as pltpu
from jax.sharding import PartitionSpec as P

HEAD_SIZE = 128
GROUP = 4
SPAN = 192
SLOTS = 32
N_CTX = 16
CHIPS = 8
TOKENS = 384
KEY_BLOCK = 384
KEY_BLOCKS = 16
OWN_BLOCKS = 8
ROWS = GROUP * SPAN
FEATURES = 256
SCALE = HEAD_SIZE ** (-0.5)
EXP2_SCALE = SCALE * 1.4426950408889634
F32 = jnp.float32
BF16 = jnp.bfloat16
VMEM_BYTES = 58 * 1024 * 1024


def ctx_move(value, dx, dz, dc):
    pairs = []
    for i in range(N_CTX):
        x, z, c = i // 8, (i // 2) % 4, i % 2
        pairs.append((i, ((x ^ dx) * 4 + (z + dz) % 4) * 2 + (c ^ dc)))
    return lax.ppermute(value, "ctx", pairs)


STEPS = ((0, 0), (1, 0), (0, 3), (0, 1), (1, 3), (1, 1), (0, 2), (1, 2))


def gather_over_ctx(own):
    across = ctx_move(own, 1, 0, 0)
    up0 = ctx_move(own, 0, 1, 0)
    down0 = ctx_move(own, 0, 3, 0)
    up1 = ctx_move(across, 0, 1, 0)
    down1 = ctx_move(across, 0, 3, 0)
    far0 = ctx_move(up0, 0, 1, 0)
    far1 = ctx_move(down1, 0, 3, 0)
    mine = [own, across, up0, down0, up1, down1, far0, far1]
    return mine + [swap(piece) for piece in mine]


def swap(value):
    return ctx_move(value, 0, 0, 1)


def source_of(ids, step, other_core):
    x, z, c = ids[0] // 8, (ids[0] // 2) % 4, ids[0] % 2
    dx, dz = STEPS[step]
    return ((x ^ dx) * 4 + (z + dz) % 4) * 2 + (c ^ other_core)


def nt(a, b):
    return lax.dot_general(a, b, (((1,), (1,)), ((), ())), preferred_element_type=F32)


def nn(a, b):
    return lax.dot_general(a, b, (((1,), (0,)), ((), ())), preferred_element_type=F32)


def key_rows(b):
    return pl.ds(pl.multiple_of(b * KEY_BLOCK, KEY_BLOCK), KEY_BLOCK)


def span_rows(n):
    return pl.ds(pl.multiple_of(n * SPAN, SPAN), SPAN)


def heads_down(value, half):
    rows = value[half * SPAN : (half + 1) * SPAN]
    return jnp.concatenate(
        [rows[:, h * HEAD_SIZE : (h + 1) * HEAD_SIZE] for h in range(GROUP)], axis=0
    )


def row_in_span(shape, dim):
    row = lax.broadcasted_iota(jnp.int32, shape, dim)
    within = row
    for h in range(1, GROUP):
        within = within - jnp.where(row >= h * SPAN, SPAN, 0)
    return within


def forward_kernel(ids, spans, q_ref, *rest):
    kv_refs, (attn_ref, lse_ref, ks, vs, qs, acc, tops, sums) = rest[:16], rest[16:]
    for piece in range(16):
        source = source_of(ids, piece % 8, piece // 8)
        for half in range(2):
            at, rows = span_rows(spans[source, half]), pl.ds(half * SPAN, SPAN)
            ks[at, :] = kv_refs[piece][rows, :HEAD_SIZE]
            vs[at, :] = kv_refs[piece][rows, HEAD_SIZE:]
    for half in range(2):
        qs[half] = heads_down(q_ref[...], half)

    for half in range(2):
        span = spans[ids[0], half]
        last = span // 2

        def step(b, masked):
            s = nt(qs[half], ks[key_rows(b), :])
            if masked:
                seen = span * SPAN + row_in_span((ROWS, 1), 0) - b * KEY_BLOCK
                s = jnp.where(lax.broadcasted_iota(jnp.int32, s.shape, 1) > seen, -1e30, s)
            old = tops[...]
            new = jnp.maximum(old, jnp.max(s, axis=1, keepdims=True))
            shrink = jnp.exp2((old - new) * EXP2_SCALE)
            tops[...] = new
            total, low = 0.0, []
            for k in range(0, KEY_BLOCK, HEAD_SIZE):
                p = jnp.exp2((s[:, k : k + HEAD_SIZE] - new) * EXP2_SCALE)
                total = total + p
                low.append(p.astype(BF16))
            sums[...] = sums[...] * shrink + total
            acc[...] = acc[...] * shrink + nn(jnp.concatenate(low, axis=1), vs[key_rows(b), :])

        tops[...] = jnp.full(tops.shape, -1e30, F32)
        sums[...] = jnp.zeros(sums.shape, F32)
        acc[...] = jnp.zeros(acc.shape, F32)

        @pl.loop(0, last)
        def _(b):
            step(b, False)

        step(last, True)
        total = jnp.sum(sums[...], axis=1, keepdims=True)
        attn = (acc[...] * (1.0 / total)).astype(BF16)
        for h in range(GROUP):
            attn_ref[pl.ds(half * SPAN, SPAN), pl.ds(h * HEAD_SIZE, HEAD_SIZE)] = attn[
                h * SPAN : (h + 1) * SPAN
            ]
        lse_ref[half] = (tops[...] * EXP2_SCALE + jnp.log2(total)).T[:8]


def smem():
    return pl.BlockSpec(memory_space=pltpu.SMEM)


def vmem():
    return pl.BlockSpec(memory_space=pltpu.VMEM)


def call(kernel, inputs, outputs, scratch, flops, name):
    bytes_moved = sum(x.size * x.dtype.itemsize for x in list(inputs) + list(outputs))
    return pl.pallas_call(
        kernel,
        out_shape=outputs,
        in_specs=[smem(), smem()] + [vmem()] * (len(inputs) - 2),
        out_specs=(vmem(),) * len(outputs),
        scratch_shapes=scratch,
        compiler_params=pltpu.CompilerParams(vmem_limit_bytes=VMEM_BYTES),
        cost_estimate=pl.CostEstimate(flops=flops, bytes_accessed=bytes_moved, transcendentals=0),
        name=name,
    )(*inputs)


def forward(ids, span_map, query, kv_pieces):
    keys = pltpu.VMEM((KEY_BLOCKS * KEY_BLOCK, HEAD_SIZE), BF16)
    rows = pltpu.VMEM((ROWS, HEAD_SIZE), F32)
    return call(
        forward_kernel,
        (ids, span_map, query, *kv_pieces),
        (
            jax.ShapeDtypeStruct(query.shape, BF16),
            jax.ShapeDtypeStruct((2, 8, ROWS), F32),
        ),
        [keys, keys, pltpu.VMEM((2, ROWS, HEAD_SIZE), BF16), rows, rows, rows],
        10_000_000_000,
        "forward",
    )


def backward_kernel(ids, spans, *rest):
    (q_own, q_other, do_own, do_other, attn_own, attn_other, lse_own, lse_other), rest = (
        rest[:8],
        rest[8:],
    )
    kv_refs, (part_ref, ks, vs, qs, dos, lse, delta, acc_k, acc_v, slot, rank, seen, order) = (
        rest[:8],
        rest[8:],
    )
    core = ids[0] % 2
    for s in range(SLOTS):
        slot[s] = 0
    for chip in range(CHIPS):
        for half in range(2):
            slot[spans[chip * 2 + core, half]] = chip * 2 + half + 1
    count = jnp.int32(0)
    for s in range(SLOTS):
        order[count] = s
        rank[s] = count
        count = count + jnp.minimum(slot[s], 1)
        seen[s] = count

    for piece in range(8):
        source = source_of(ids, piece, 0)
        for half in range(2):
            at, rows = span_rows(rank[spans[source, half]]), pl.ds(half * SPAN, SPAN)
            ks[at, :] = kv_refs[piece][rows, :HEAD_SIZE]
            vs[at, :] = kv_refs[piece][rows, HEAD_SIZE:]
    sides = ((q_own, do_own, attn_own, lse_own), (q_other, do_other, attn_other, lse_other))
    for side, (q_ref, do_ref, attn_ref, lse_ref) in enumerate(sides):
        product = do_ref[...].astype(F32) * attn_ref[...].astype(F32)
        for half in range(2):
            qs[side * 2 + half] = heads_down(q_ref[...], half)
            dos[side * 2 + half] = heads_down(do_ref[...], half)
            lse[side * 2 + half] = lse_ref[half, :1]
            delta[side * 2 + half] = jnp.sum(heads_down(product, half).T, axis=0, keepdims=True)

    def tile(b, group, span, masked):
        s = nt(ks[key_rows(b), :], qs[group])
        if masked:
            row = lax.broadcasted_iota(jnp.int32, (KEY_BLOCK, 1), 0)
            at = jnp.where(row < SPAN, order[b * 2] * SPAN, (order[b * 2 + 1] - 1) * SPAN) + row
            s = jnp.where(at > span * SPAN + row_in_span((1, ROWS), 1), -1e30, s)
        p = jnp.exp2(s * EXP2_SCALE - lse[group])
        d_p = nt(vs[key_rows(b), :], dos[group])
        d_s = (p * (d_p - delta[group])).astype(BF16)
        acc_k[...] += nn(d_s, qs[group])
        acc_v[...] += nn(p.astype(BF16), dos[group])

    @pl.loop(0, OWN_BLOCKS)
    def _(b):
        acc_k[...] = jnp.zeros(acc_k.shape, F32)
        acc_v[...] = jnp.zeros(acc_v.shape, F32)

        @pl.loop(0, 4)
        def _(group):
            span = spans[ids[0] ^ (group // 2), group % 2]
            last = (seen[span] + 1) // 2 - 1

            @pl.when(b < last)
            def _():
                tile(b, group, span, False)

            @pl.when(b == last)
            def _():
                tile(b, group, span, True)

        d_key = (acc_k[...] * SCALE).astype(BF16)
        d_value = acc_v[...].astype(BF16)
        for n in range(2):
            at = slot[order[b * 2 + n]] - 1
            part_ref[at, :, :HEAD_SIZE] = d_key[n * SPAN : (n + 1) * SPAN]
            part_ref[at, :, HEAD_SIZE:] = d_value[n * SPAN : (n + 1) * SPAN]


def backward(ids, span_map, sides, kv_pieces):
    keys = pltpu.VMEM((OWN_BLOCKS * KEY_BLOCK, HEAD_SIZE), BF16)
    rows = pltpu.VMEM((4, ROWS, HEAD_SIZE), BF16)
    stats = pltpu.VMEM((4, 1, ROWS), F32)
    sums = pltpu.VMEM((KEY_BLOCK, HEAD_SIZE), F32)
    table = pltpu.SMEM((SLOTS,), jnp.int32)
    (part,) = call(
        backward_kernel,
        (ids, span_map, *sides, *kv_pieces),
        (jax.ShapeDtypeStruct((2 * CHIPS, SPAN, 2 * HEAD_SIZE), BF16),),
        [keys, keys, rows, rows, stats, stats, sums, sums, table, table, table, table],
        12_000_000_000,
        "backward",
    )
    return part


def blocks_by_owner(owners, n, found):
    for b in range(N_CTX):
        found[owners[n, b]] = b


def feature_block(ref, b):
    return ref[:, pl.ds(pl.multiple_of(b * FEATURES, FEATURES), FEATURES)]


def out_kernel(columns, ids, owners, attn_ref, grad_ref, own_ref, other_ref, found):
    core = ids[0] % 2
    blocks_by_owner(owners, 2, found)
    attn_t = attn_ref[:, columns].astype(F32).T.astype(BF16)
    for out_ref, at in ((other_ref, 1 - core), (own_ref, core)):
        for chip in range(CHIPS):
            out_ref[chip] = nn(attn_t, feature_block(grad_ref, found[chip * 2 + at])).astype(BF16)


def out_gradient(ids, owner_map, attn, grad, half):
    part = jax.ShapeDtypeStruct((CHIPS, FEATURES, FEATURES), BF16)
    columns = slice(half * FEATURES, (half + 1) * FEATURES)

    def kernel(*refs):
        out_kernel(columns, *refs)

    return call(
        kernel,
        (ids, owner_map, attn, grad),
        (part, part),
        [pltpu.SMEM((N_CTX,), jnp.int32)],
        800_000_000,
        f"out_gradient_{half}",
    )


def kv_kernel(ids, owners, parts_ref, hidden_ref, own_ref, other_ref, found_k, found_v):
    core = ids[0] % 2
    blocks_by_owner(owners, 0, found_k)
    blocks_by_owner(owners, 1, found_v)
    total = jnp.sum(parts_ref[...].astype(F32), axis=0)
    both = []
    for n in range(2):
        t = total[:, n * HEAD_SIZE : (n + 1) * HEAD_SIZE].T
        high = t.astype(BF16)
        both.append(jnp.concatenate([high, (t - high.astype(F32)).astype(BF16)], axis=0))
    for out_ref, at in ((other_ref, 1 - core), (own_ref, core)):
        for chip in range(CHIPS):
            for n, found in enumerate((found_k, found_v)):
                block = nn(both[n], feature_block(hidden_ref, found[chip * 2 + at]))
                out_ref[chip, n * HEAD_SIZE : (n + 1) * HEAD_SIZE, :] = (
                    block[:HEAD_SIZE] + block[HEAD_SIZE:]
                ).astype(BF16)


def kv_gradient(ids, owner_map, parts, hidden):
    part = jax.ShapeDtypeStruct((CHIPS, 2 * HEAD_SIZE, FEATURES), BF16)
    found = pltpu.SMEM((N_CTX,), jnp.int32)
    return call(
        kv_kernel,
        (ids, owner_map, parts, hidden),
        (part, part),
        [found, found],
        1_600_000_000,
        "kv_gradient",
    )


SAME_CORE = [[c + 2 * chip for chip in range(CHIPS)] for c in range(2)]


def exchange(parts):
    return lax.all_to_all(parts, "ctx", 0, 0, tiled=True, axis_index_groups=SAME_CORE)


def chip_sum(own, other):
    return (own.astype(F32) + swap(other).astype(F32)).astype(BF16)


def after(value, *earlier):
    return lax.optimization_barrier((value, *earlier))[0]


def per_device(hidden_in, query, key, value, out_weight, grad_out, span_map, owner_map):
    ids = jnp.stack([lax.axis_index("ctx"), lax.axis_index("head")]).astype(jnp.int32)
    grad = lax.all_gather(grad_out, "head", axis=1, tiled=True)
    hidden = lax.all_gather(after(hidden_in, grad), "head", axis=1, tiled=True)
    kv_pieces = gather_over_ctx(jnp.concatenate([key, value], axis=1))
    query_other = swap(query)
    attn, lse = forward(ids, span_map, query, kv_pieces)
    d_attn = nt(grad, out_weight).astype(BF16)
    out_first = exchange(chip_sum(*out_gradient(ids, owner_map, attn, grad, 0)))
    sides = (query, query_other, d_attn, swap(d_attn), attn, swap(attn), lse, swap(lse))
    dkv = backward(ids, span_map, sides, kv_pieces[:8])
    attn_late = after(attn, dkv)
    dkv = exchange(dkv).reshape(CHIPS, TOKENS, 2 * HEAD_SIZE)
    out_second = chip_sum(*out_gradient(ids, owner_map, attn_late, grad, 1))
    out_second = exchange(after(out_second, dkv))
    kv_total = exchange(chip_sum(*kv_gradient(ids, owner_map, dkv, hidden)))
    kv_total = jnp.sum(kv_total.astype(F32), axis=0)
    out_total = jnp.concatenate(
        [jnp.sum(part.astype(F32), axis=0) for part in (out_first, out_second)], axis=0
    )
    return kv_total[:HEAD_SIZE].T, kv_total[HEAD_SIZE:].T, out_total


def solution(mesh):
    return jax.shard_map(
        per_device,
        mesh=mesh,
        in_specs=(
            P("ctx", "head"),
            P("ctx", "head"),
            P("ctx", "head"),
            P("ctx", "head"),
            P("head", None),
            P("ctx", "head"),
            P(),
            P(),
        ),
        out_specs=(P("ctx", "head"), P("ctx", "head"), P("head", "ctx")),
        check_vma=False,
    )
```

```python
import jax
import jax.numpy as jnp
from jax import lax
from jax.experimental import pallas as pl
from jax.experimental.pallas import tpu as pltpu
from jax.sharding import PartitionSpec as P

HEAD_SIZE = 128
GROUP = 4
SPAN = 192
SLOTS = 32
N_CTX = 16
CHIPS = 8
TOKENS = 384
KEY_BLOCK = 384
KEY_BLOCKS = 16
OWN_BLOCKS = 8
ROWS = GROUP * SPAN
FEATURES = 256
HEAD_COLUMNS = 512
SCALE = HEAD_SIZE ** (-0.5)
EXP2_SCALE = SCALE * 1.4426950408889634
F32 = jnp.float32
BF16 = jnp.bfloat16
VMEM_BYTES = 58 * 1024 * 1024


def ctx_move(value, dx, dz, dc):
    pairs = []
    for i in range(N_CTX):
        x, z, c = i // 8, (i // 2) % 4, i % 2
        pairs.append((i, ((x ^ dx) * 4 + (z + dz) % 4) * 2 + (c ^ dc)))
    return lax.ppermute(value, "ctx", pairs)


STEPS = ((0, 0), (1, 0), (0, 3), (0, 1), (1, 3), (1, 1), (0, 2), (1, 2))


def gather_over_ctx(own):
    across = ctx_move(own, 1, 0, 0)
    up0 = ctx_move(own, 0, 1, 0)
    down0 = ctx_move(own, 0, 3, 0)
    up1 = ctx_move(across, 0, 1, 0)
    down1 = ctx_move(across, 0, 3, 0)
    far0 = ctx_move(up0, 0, 1, 0)
    far1 = ctx_move(down1, 0, 3, 0)
    mine = [own, across, up0, down0, up1, down1, far0, far1]
    return mine + [swap(piece) for piece in mine]


def swap(value):
    return ctx_move(value, 0, 0, 1)


def source_of(ids, step, other_core):
    x, z, c = ids[0] // 8, (ids[0] // 2) % 4, ids[0] % 2
    dx, dz = STEPS[step]
    return ((x ^ dx) * 4 + (z + dz) % 4) * 2 + (c ^ other_core)


def nt(a, b):
    return lax.dot_general(a, b, (((1,), (1,)), ((), ())), preferred_element_type=F32)


def nn(a, b):
    return lax.dot_general(a, b, (((1,), (0,)), ((), ())), preferred_element_type=F32)


def key_rows(b):
    return pl.ds(pl.multiple_of(b * KEY_BLOCK, KEY_BLOCK), KEY_BLOCK)


def span_rows(n):
    return pl.ds(pl.multiple_of(n * SPAN, SPAN), SPAN)


def heads_down(value, half):
    rows = value[half * SPAN : (half + 1) * SPAN]
    return jnp.concatenate(
        [rows[:, h * HEAD_SIZE : (h + 1) * HEAD_SIZE] for h in range(GROUP)], axis=0
    )


def row_in_span(shape, dim):
    row = lax.broadcasted_iota(jnp.int32, shape, dim)
    within = row
    for h in range(1, GROUP):
        within = within - jnp.where(row >= h * SPAN, SPAN, 0)
    return within


def forward_kernel(ids, spans, q_ref, *rest):
    kv_refs, (attn_ref, lse_ref, ks, vs, qs, acc, tops, sums) = rest[:16], rest[16:]
    for piece in range(16):
        source = source_of(ids, piece % 8, piece // 8)
        for half in range(2):
            at, rows = span_rows(spans[source, half]), pl.ds(half * SPAN, SPAN)
            ks[at, :] = kv_refs[piece][rows, :HEAD_SIZE]
            vs[at, :] = kv_refs[piece][rows, HEAD_SIZE:]
    for half in range(2):
        qs[half] = heads_down(q_ref[...], half)

    for half in range(2):
        span = spans[ids[0], half]
        last = span // 2

        def step(b, masked):
            s = nt(qs[half], ks[key_rows(b), :])
            if masked:
                seen = span * SPAN + row_in_span((ROWS, 1), 0) - b * KEY_BLOCK
                s = jnp.where(lax.broadcasted_iota(jnp.int32, s.shape, 1) > seen, -1e30, s)
            old = tops[...]
            new = jnp.maximum(old, jnp.max(s, axis=1, keepdims=True))
            shrink = jnp.exp2((old - new) * EXP2_SCALE)
            tops[...] = new
            total, low = 0.0, []
            for k in range(0, KEY_BLOCK, HEAD_SIZE):
                p = jnp.exp2((s[:, k : k + HEAD_SIZE] - new) * EXP2_SCALE)
                total = total + p
                low.append(p.astype(BF16))
            sums[...] = sums[...] * shrink + total
            acc[...] = acc[...] * shrink + nn(jnp.concatenate(low, axis=1), vs[key_rows(b), :])

        tops[...] = jnp.full(tops.shape, -1e30, F32)
        sums[...] = jnp.zeros(sums.shape, F32)
        acc[...] = jnp.zeros(acc.shape, F32)

        @pl.loop(0, last)
        def _(b):
            step(b, False)

        step(last, True)
        total = jnp.sum(sums[...], axis=1, keepdims=True)
        attn = (acc[...] * (1.0 / total)).astype(BF16)
        for h in range(GROUP):
            attn_ref[pl.ds(half * SPAN, SPAN), pl.ds(h * HEAD_SIZE, HEAD_SIZE)] = attn[
                h * SPAN : (h + 1) * SPAN
            ]
        lse_ref[half] = (tops[...] * EXP2_SCALE + jnp.log2(total)).T[:8]


def smem():
    return pl.BlockSpec(memory_space=pltpu.SMEM)


def vmem():
    return pl.BlockSpec(memory_space=pltpu.VMEM)


def call(kernel, inputs, outputs, scratch, flops, name):
    return pl.pallas_call(
        kernel,
        out_shape=outputs,
        in_specs=[smem(), smem()] + [vmem()] * (len(inputs) - 2),
        out_specs=(vmem(),) * len(outputs),
        scratch_shapes=scratch,
        compiler_params=pltpu.CompilerParams(vmem_limit_bytes=VMEM_BYTES),
        cost_estimate=pl.CostEstimate(flops=flops, bytes_accessed=1024, transcendentals=0),
        name=name,
    )(*inputs)


def forward(ids, span_map, query, kv_pieces):
    keys = pltpu.VMEM((KEY_BLOCKS * KEY_BLOCK, HEAD_SIZE), BF16)
    rows = pltpu.VMEM((ROWS, HEAD_SIZE), F32)
    return call(
        forward_kernel,
        (ids, span_map, query, *kv_pieces),
        (
            jax.ShapeDtypeStruct(query.shape, BF16),
            jax.ShapeDtypeStruct((2, 8, ROWS), F32),
        ),
        [keys, keys, pltpu.VMEM((2, ROWS, HEAD_SIZE), BF16), rows, rows, rows],
        1_000_000,
        "forward",
    )


def backward_kernel(ids, spans, *rest):
    (q_own, q_other, do_own, do_other, attn_own, attn_other, lse_own, lse_other), rest = (
        rest[:8],
        rest[8:],
    )
    kv_refs, (part_ref, ks, vs, qs, dos, lse, delta, acc_k, acc_v, slot, rank, seen, order) = (
        rest[:8],
        rest[8:],
    )
    core = ids[0] % 2
    for s in range(SLOTS):
        slot[s] = 0
    for chip in range(CHIPS):
        for half in range(2):
            slot[spans[chip * 2 + core, half]] = chip * 2 + half + 1
    count = jnp.int32(0)
    for s in range(SLOTS):
        order[count] = s
        rank[s] = count
        count = count + jnp.minimum(slot[s], 1)
        seen[s] = count

    for piece in range(8):
        source = source_of(ids, piece, 0)
        for half in range(2):
            at, rows = span_rows(rank[spans[source, half]]), pl.ds(half * SPAN, SPAN)
            ks[at, :] = kv_refs[piece][rows, :HEAD_SIZE]
            vs[at, :] = kv_refs[piece][rows, HEAD_SIZE:]
    sides = ((q_own, do_own, attn_own, lse_own), (q_other, do_other, attn_other, lse_other))
    for side, (q_ref, do_ref, attn_ref, lse_ref) in enumerate(sides):
        product = do_ref[...].astype(F32) * attn_ref[...].astype(F32)
        for half in range(2):
            qs[side * 2 + half] = heads_down(q_ref[...], half)
            dos[side * 2 + half] = heads_down(do_ref[...], half)
            lse[side * 2 + half] = lse_ref[half, :1]
            delta[side * 2 + half] = jnp.sum(heads_down(product, half).T, axis=0, keepdims=True)

    def tile(b, group, span, masked):
        s = nt(ks[key_rows(b), :], qs[group])
        if masked:
            row = lax.broadcasted_iota(jnp.int32, (KEY_BLOCK, 1), 0)
            at = jnp.where(row < SPAN, order[b * 2] * SPAN, (order[b * 2 + 1] - 1) * SPAN) + row
            s = jnp.where(at > span * SPAN + row_in_span((1, ROWS), 1), -1e30, s)
        p = jnp.exp2(s * EXP2_SCALE - lse[group])
        d_p = nt(vs[key_rows(b), :], dos[group])
        d_s = (p * (d_p - delta[group])).astype(BF16)
        acc_k[...] += nn(d_s, qs[group])
        acc_v[...] += nn(p.astype(BF16), dos[group])

    @pl.loop(0, OWN_BLOCKS)
    def _(b):
        acc_k[...] = jnp.zeros(acc_k.shape, F32)
        acc_v[...] = jnp.zeros(acc_v.shape, F32)

        @pl.loop(0, 4)
        def _(group):
            span = spans[ids[0] ^ (group // 2), group % 2]
            last = (seen[span] + 1) // 2 - 1

            @pl.when(b < last)
            def _():
                tile(b, group, span, False)

            @pl.when(b == last)
            def _():
                tile(b, group, span, True)

        d_key = (acc_k[...] * SCALE).astype(BF16)
        d_value = acc_v[...].astype(BF16)
        for n in range(2):
            at = slot[order[b * 2 + n]] - 1
            part_ref[at, :, :HEAD_SIZE] = d_key[n * SPAN : (n + 1) * SPAN]
            part_ref[at, :, HEAD_SIZE:] = d_value[n * SPAN : (n + 1) * SPAN]


def backward(ids, span_map, sides, kv_pieces):
    keys = pltpu.VMEM((OWN_BLOCKS * KEY_BLOCK, HEAD_SIZE), BF16)
    rows = pltpu.VMEM((4, ROWS, HEAD_SIZE), BF16)
    stats = pltpu.VMEM((4, 1, ROWS), F32)
    sums = pltpu.VMEM((KEY_BLOCK, HEAD_SIZE), F32)
    table = pltpu.SMEM((SLOTS,), jnp.int32)
    (part,) = call(
        backward_kernel,
        (ids, span_map, *sides, *kv_pieces),
        (jax.ShapeDtypeStruct((2 * CHIPS, SPAN, 2 * HEAD_SIZE), BF16),),
        [keys, keys, rows, rows, stats, stats, sums, sums, table, table, table, table],
        1_000_000,
        "backward",
    )
    return part


def blocks_by_owner(owners, n, found):
    for b in range(N_CTX):
        found[owners[n, b]] = b


def feature_block(ref, b):
    return ref[:, pl.ds(pl.multiple_of(b * FEATURES, FEATURES), FEATURES)]


def out_kernel(ids, owners, attn_ref, grad_ref, own_ref, other_ref, found):
    core = ids[0] % 2
    blocks_by_owner(owners, 2, found)
    attn_t = attn_ref[...].astype(F32).T.astype(BF16)
    for out_ref, at in ((other_ref, 1 - core), (own_ref, core)):
        for chip in range(CHIPS):
            out_ref[chip] = nn(attn_t, feature_block(grad_ref, found[chip * 2 + at])).astype(BF16)


def out_gradient(ids, owner_map, attn, grad):
    part = jax.ShapeDtypeStruct((CHIPS, HEAD_COLUMNS, FEATURES), BF16)
    return call(
        out_kernel,
        (ids, owner_map, attn, grad),
        (part, part),
        [pltpu.SMEM((N_CTX,), jnp.int32)],
        3_200_000_000,
        "out_gradient",
    )


def kv_kernel(ids, owners, parts_ref, hidden_ref, own_ref, other_ref, found_k, found_v):
    core = ids[0] % 2
    blocks_by_owner(owners, 0, found_k)
    blocks_by_owner(owners, 1, found_v)
    total = jnp.sum(parts_ref[...].astype(F32), axis=0)
    both = []
    for n in range(2):
        t = total[:, n * HEAD_SIZE : (n + 1) * HEAD_SIZE].T
        high = t.astype(BF16)
        both.append(jnp.concatenate([high, (t - high.astype(F32)).astype(BF16)], axis=0))
    for out_ref, at in ((other_ref, 1 - core), (own_ref, core)):
        for chip in range(CHIPS):
            for n, found in enumerate((found_k, found_v)):
                block = nn(both[n], feature_block(hidden_ref, found[chip * 2 + at]))
                out_ref[chip, n * HEAD_SIZE : (n + 1) * HEAD_SIZE, :] = (
                    block[:HEAD_SIZE] + block[HEAD_SIZE:]
                ).astype(BF16)


def kv_gradient(ids, owner_map, parts, hidden):
    part = jax.ShapeDtypeStruct((CHIPS, 2 * HEAD_SIZE, FEATURES), BF16)
    found = pltpu.SMEM((N_CTX,), jnp.int32)
    return call(
        kv_kernel,
        (ids, owner_map, parts, hidden),
        (part, part),
        [found, found],
        1_000_000,
        "kv_gradient",
    )


SAME_CORE = [[c + 2 * chip for chip in range(CHIPS)] for c in range(2)]


def exchange(parts):
    return lax.all_to_all(parts, "ctx", 0, 0, tiled=True, axis_index_groups=SAME_CORE)


def chip_sum(own, other):
    return (own.astype(F32) + swap(other).astype(F32)).astype(BF16)


def after(value, *earlier):
    return lax.optimization_barrier((value, *earlier))[0]


def per_device(hidden_in, query, key, value, out_weight, grad_out, span_map, owner_map):
    ids = jnp.stack([lax.axis_index("ctx"), lax.axis_index("head")]).astype(jnp.int32)
    grad = lax.all_gather(grad_out, "head", axis=1, tiled=True)
    kv_pieces = gather_over_ctx(jnp.concatenate([key, value], axis=1))
    query_other = swap(query)
    attn, lse = forward(ids, span_map, after(query, query_other), kv_pieces)
    hidden = lax.all_gather(after(hidden_in, attn), "head", axis=1, tiled=True)
    d_attn = nt(after(grad, attn), out_weight).astype(BF16)
    sides = (query, query_other, d_attn, swap(d_attn), attn, swap(attn), lse, swap(lse))
    dkv = backward(ids, span_map, sides, kv_pieces[:8])
    attn_late = after(attn, dkv)
    dkv = exchange(dkv).reshape(CHIPS, TOKENS, 2 * HEAD_SIZE)
    out_parts = chip_sum(*out_gradient(ids, owner_map, attn_late, grad))
    out_parts = exchange(after(out_parts, dkv))
    kv_total = chip_sum(*kv_gradient(ids, owner_map, dkv, hidden))
    kv_total = exchange(after(kv_total, out_parts))
    kv_total = jnp.sum(kv_total.astype(F32), axis=0)
    out_total = jnp.sum(out_parts.astype(F32), axis=0)
    return kv_total[:HEAD_SIZE].T, kv_total[HEAD_SIZE:].T, out_total


def solution(mesh):
    return jax.shard_map(
        per_device,
        mesh=mesh,
        in_specs=(
            P("ctx", "head"),
            P("ctx", "head"),
            P("ctx", "head"),
            P("ctx", "head"),
            P("head", None),
            P("ctx", "head"),
            P(),
            P(),
        ),
        out_specs=(P("ctx", "head"), P("ctx", "head"), P("head", "ctx")),
        check_vma=False,
    )
```

```python
import jax
import jax.numpy as jnp
from jax import lax
from jax.experimental import pallas as pl
from jax.experimental.pallas import tpu as pltpu
from jax.sharding import PartitionSpec as P

HEAD_SIZE = 128
GROUP = 4
SPAN = 192
SLOTS = 32
N_CTX = 16
CHIPS = 8
TOKENS = 384
KEY_BLOCK = 384
KEY_BLOCKS = 16
OUT_FLOPS = 8_000_000_000
OWN_BLOCKS = 8
WIDE = 3
ROWS = GROUP * SPAN
FEATURES = 256
HEAD_COLUMNS = 512
SCALE = HEAD_SIZE ** (-0.5)
EXP2_SCALE = SCALE * 1.4426950408889634
F32 = jnp.float32
BF16 = jnp.bfloat16
VMEM_BYTES = 58 * 1024 * 1024


def ctx_move(value, dx, dz, dc):
    pairs = []
    for i in range(N_CTX):
        x, z, c = i // 8, (i // 2) % 4, i % 2
        pairs.append((i, ((x ^ dx) * 4 + (z + dz) % 4) * 2 + (c ^ dc)))
    return lax.ppermute(value, "ctx", pairs)


STEPS = ((0, 0), (1, 0), (0, 3), (0, 1), (1, 3), (1, 1), (0, 2), (1, 2))


def gather_over_ctx(own):
    across = ctx_move(own, 1, 0, 0)
    up0 = ctx_move(own, 0, 1, 0)
    down0 = ctx_move(own, 0, 3, 0)
    up1 = ctx_move(across, 0, 1, 0)
    down1 = ctx_move(across, 0, 3, 0)
    far0 = ctx_move(up0, 0, 1, 0)
    far1 = ctx_move(down1, 0, 3, 0)
    mine = [own, across, up0, down0, up1, down1, far0, far1]
    return mine + [swap(piece) for piece in mine]


def swap(value):
    return ctx_move(value, 0, 0, 1)


def source_of(ids, step, other_core):
    x, z, c = ids[0] // 8, (ids[0] // 2) % 4, ids[0] % 2
    dx, dz = STEPS[step]
    return ((x ^ dx) * 4 + (z + dz) % 4) * 2 + (c ^ other_core)


def nt(a, b):
    return lax.dot_general(a, b, (((1,), (1,)), ((), ())), preferred_element_type=F32)


def nn(a, b):
    return lax.dot_general(a, b, (((1,), (0,)), ((), ())), preferred_element_type=F32)


def key_rows(b):
    return pl.ds(pl.multiple_of(b * KEY_BLOCK, KEY_BLOCK), KEY_BLOCK)


def span_rows(n):
    return pl.ds(pl.multiple_of(n * SPAN, SPAN), SPAN)


def heads_down(value, half):
    rows = value[half * SPAN : (half + 1) * SPAN]
    return jnp.concatenate(
        [rows[:, h * HEAD_SIZE : (h + 1) * HEAD_SIZE] for h in range(GROUP)], axis=0
    )


def row_in_span(shape, dim):
    row = lax.broadcasted_iota(jnp.int32, shape, dim)
    within = row
    for h in range(1, GROUP):
        within = within - jnp.where(row >= h * SPAN, SPAN, 0)
    return within


def forward_kernel(ids, spans, q_ref, *rest):
    kv_refs, (attn_ref, lse_ref, ks, vs, qs, acc, tops, sums) = rest[:16], rest[16:]
    for piece in range(16):
        source = source_of(ids, piece % 8, piece // 8)
        for half in range(2):
            at, rows = span_rows(spans[source, half]), pl.ds(half * SPAN, SPAN)
            ks[at, :] = kv_refs[piece][rows, :HEAD_SIZE]
            vs[at, :] = kv_refs[piece][rows, HEAD_SIZE:]
    for half in range(2):
        qs[half] = heads_down(q_ref[...], half)

    for half in range(2):
        span = spans[ids[0], half]
        last = span // 2

        def step(b, masked):
            s = nt(qs[half], ks[key_rows(b), :])
            if masked:
                seen = span * SPAN + row_in_span((ROWS, 1), 0) - b * KEY_BLOCK
                s = jnp.where(lax.broadcasted_iota(jnp.int32, s.shape, 1) > seen, -1e30, s)
            old = tops[...]
            new = jnp.maximum(old, jnp.max(s, axis=1, keepdims=True))
            shrink = jnp.exp2((old - new) * EXP2_SCALE)
            tops[...] = new
            total, low = 0.0, []
            for k in range(0, KEY_BLOCK, HEAD_SIZE):
                p = jnp.exp2((s[:, k : k + HEAD_SIZE] - new) * EXP2_SCALE)
                total = total + p
                low.append(p.astype(BF16))
            sums[...] = sums[...] * shrink + total
            acc[...] = acc[...] * shrink + nn(jnp.concatenate(low, axis=1), vs[key_rows(b), :])

        tops[...] = jnp.full(tops.shape, -1e30, F32)
        sums[...] = jnp.zeros(sums.shape, F32)
        acc[...] = jnp.zeros(acc.shape, F32)

        @pl.loop(0, last)
        def _(b):
            step(b, False)

        step(last, True)
        total = jnp.sum(sums[...], axis=1, keepdims=True)
        attn = (acc[...] * (1.0 / total)).astype(BF16)
        for h in range(GROUP):
            attn_ref[pl.ds(half * SPAN, SPAN), pl.ds(h * HEAD_SIZE, HEAD_SIZE)] = attn[
                h * SPAN : (h + 1) * SPAN
            ]
        lse_ref[half] = (tops[...] * EXP2_SCALE + jnp.log2(total)).T[:8]


def smem():
    return pl.BlockSpec(memory_space=pltpu.SMEM)


def vmem():
    return pl.BlockSpec(memory_space=pltpu.VMEM)


def call(kernel, inputs, outputs, scratch, flops, name):
    return pl.pallas_call(
        kernel,
        out_shape=outputs,
        in_specs=[smem(), smem()] + [vmem()] * (len(inputs) - 2),
        out_specs=(vmem(),) * len(outputs),
        scratch_shapes=scratch,
        compiler_params=pltpu.CompilerParams(vmem_limit_bytes=VMEM_BYTES),
        cost_estimate=pl.CostEstimate(flops=flops, bytes_accessed=1024, transcendentals=0),
        name=name,
    )(*inputs)


def forward(ids, span_map, query, kv_pieces):
    keys = pltpu.VMEM((KEY_BLOCKS * KEY_BLOCK, HEAD_SIZE), BF16)
    rows = pltpu.VMEM((ROWS, HEAD_SIZE), F32)
    return call(
        forward_kernel,
        (ids, span_map, query, *kv_pieces),
        (
            jax.ShapeDtypeStruct(query.shape, BF16),
            jax.ShapeDtypeStruct((2, 8, ROWS), F32),
        ),
        [keys, keys, pltpu.VMEM((2, ROWS, HEAD_SIZE), BF16), rows, rows, rows],
        1_000_000,
        "forward",
    )


def backward_kernel(ids, spans, *rest):
    (q_own, q_other, do_own, do_other, attn_own, attn_other, lse_own, lse_other), rest = (
        rest[:8],
        rest[8:],
    )
    kv_refs, (part_ref, ks, vs, qs, dos, lse, delta, acc_k, acc_v, slot, rank, seen, order) = (
        rest[:8],
        rest[8:],
    )
    core = ids[0] % 2
    for s in range(SLOTS):
        slot[s] = 0
    for chip in range(CHIPS):
        for half in range(2):
            slot[spans[chip * 2 + core, half]] = chip * 2 + half + 1
    count = jnp.int32(0)
    for s in range(SLOTS):
        order[count] = s
        rank[s] = count
        count = count + jnp.minimum(slot[s], 1)
        seen[s] = count

    for piece in range(8):
        source = source_of(ids, piece, 0)
        for half in range(2):
            at, rows = span_rows(rank[spans[source, half]]), pl.ds(half * SPAN, SPAN)
            ks[at, :] = kv_refs[piece][rows, :HEAD_SIZE]
            vs[at, :] = kv_refs[piece][rows, HEAD_SIZE:]
    sides = ((q_own, do_own, attn_own, lse_own), (q_other, do_other, attn_other, lse_other))
    for side, (q_ref, do_ref, attn_ref, lse_ref) in enumerate(sides):
        product = do_ref[...].astype(F32) * attn_ref[...].astype(F32)
        for half in range(2):
            qs[side * 2 + half] = heads_down(q_ref[...], half)
            dos[side * 2 + half] = heads_down(do_ref[...], half)
            lse[side * 2 + half] = lse_ref[half, :1]
            delta[side * 2 + half] = jnp.sum(heads_down(product, half).T, axis=0, keepdims=True)

    acc_k[...] = jnp.zeros(acc_k.shape, F32)
    acc_v[...] = jnp.zeros(acc_v.shape, F32)

    def tile(first, count, group, span, masked):
        rows = pl.ds(pl.multiple_of(first, KEY_BLOCK), count)
        s = nt(ks[rows, :], qs[group])
        if masked:
            b = first // KEY_BLOCK
            row = lax.broadcasted_iota(jnp.int32, (count, 1), 0)
            at = jnp.where(row < SPAN, order[b * 2] * SPAN, (order[b * 2 + 1] - 1) * SPAN) + row
            s = jnp.where(at > span * SPAN + row_in_span((1, ROWS), 1), -1e30, s)
        p = jnp.exp2(s * EXP2_SCALE - lse[group])
        d_p = nt(vs[rows, :], dos[group])
        d_s = (p * (d_p - delta[group])).astype(BF16)
        acc_k[rows, :] += nn(d_s, qs[group])
        acc_v[rows, :] += nn(p.astype(BF16), dos[group])

    @pl.loop(0, 4)
    def _(group):
        span = spans[ids[0] ^ (group // 2), group % 2]
        last = (seen[span] + 1) // 2 - 1
        wide = jnp.maximum(last, 0) // WIDE

        @pl.loop(0, wide)
        def _(n):
            tile(n * WIDE * KEY_BLOCK, WIDE * KEY_BLOCK, group, span, False)

        @pl.loop(wide * WIDE, last)
        def _(b):
            tile(b * KEY_BLOCK, KEY_BLOCK, group, span, False)

        @pl.when(last >= 0)
        def _():
            tile(last * KEY_BLOCK, KEY_BLOCK, group, span, True)

    for n in range(2 * CHIPS):
        at = slot[order[n]] - 1
        rows = pl.ds(n * SPAN, SPAN)
        part_ref[at, :, :HEAD_SIZE] = (acc_k[rows, :] * SCALE).astype(BF16)
        part_ref[at, :, HEAD_SIZE:] = acc_v[rows, :].astype(BF16)


def backward(ids, span_map, sides, kv_pieces):
    keys = pltpu.VMEM((OWN_BLOCKS * KEY_BLOCK, HEAD_SIZE), BF16)
    rows = pltpu.VMEM((4, ROWS, HEAD_SIZE), BF16)
    stats = pltpu.VMEM((4, 1, ROWS), F32)
    sums = pltpu.VMEM((OWN_BLOCKS * KEY_BLOCK, HEAD_SIZE), F32)
    table = pltpu.SMEM((SLOTS,), jnp.int32)
    (part,) = call(
        backward_kernel,
        (ids, span_map, *sides, *kv_pieces),
        (jax.ShapeDtypeStruct((2 * CHIPS, SPAN, 2 * HEAD_SIZE), BF16),),
        [keys, keys, rows, rows, stats, stats, sums, sums, table, table, table, table],
        1_000_000,
        "backward",
    )
    return part


def blocks_by_owner(owners, n, found):
    for b in range(N_CTX):
        found[owners[n, b]] = b


def feature_block(ref, b):
    return ref[:, pl.ds(pl.multiple_of(b * FEATURES, FEATURES), FEATURES)]


def out_kernel(ids, owners, attn_own, attn_other, grad_own, grad_other, out_ref, found):
    core = ids[0] % 2
    blocks_by_owner(owners, 2, found)
    attn_t = [ref[...].astype(F32).T.astype(BF16) for ref in (attn_own, attn_other)]
    for chip in range(CHIPS):
        b = found[chip * 2 + core]
        block = nn(attn_t[0], feature_block(grad_own, b)) + nn(
            attn_t[1], feature_block(grad_other, b)
        )
        out_ref[chip] = block.astype(BF16)


def out_gradient(ids, owner_map, attn, attn_other, grad, grad_other):
    part = jax.ShapeDtypeStruct((CHIPS, HEAD_COLUMNS, FEATURES), BF16)
    (parts,) = call(
        out_kernel,
        (ids, owner_map, attn, attn_other, grad, grad_other),
        (part,),
        [pltpu.SMEM((N_CTX,), jnp.int32)],
        OUT_FLOPS,
        "out_gradient",
    )
    return parts


def kv_kernel(ids, owners, parts_ref, hidden_ref, own_ref, other_ref, found_k, found_v):
    core = ids[0] % 2
    blocks_by_owner(owners, 0, found_k)
    blocks_by_owner(owners, 1, found_v)
    total = jnp.sum(parts_ref[...].astype(F32), axis=0)
    both = []
    for n in range(2):
        t = total[:, n * HEAD_SIZE : (n + 1) * HEAD_SIZE].T
        high = t.astype(BF16)
        both.append(jnp.concatenate([high, (t - high.astype(F32)).astype(BF16)], axis=0))
    for out_ref, at in ((other_ref, 1 - core), (own_ref, core)):
        for chip in range(CHIPS):
            for n, found in enumerate((found_k, found_v)):
                block = nn(both[n], feature_block(hidden_ref, found[chip * 2 + at]))
                out_ref[chip, n * HEAD_SIZE : (n + 1) * HEAD_SIZE, :] = (
                    block[:HEAD_SIZE] + block[HEAD_SIZE:]
                ).astype(BF16)


def kv_gradient(ids, owner_map, parts, hidden):
    part = jax.ShapeDtypeStruct((CHIPS, 2 * HEAD_SIZE, FEATURES), BF16)
    found = pltpu.SMEM((N_CTX,), jnp.int32)
    return call(
        kv_kernel,
        (ids, owner_map, parts, hidden),
        (part, part),
        [found, found],
        1_000_000,
        "kv_gradient",
    )


SAME_CORE = [[c + 2 * chip for chip in range(CHIPS)] for c in range(2)]


def exchange(parts):
    return lax.all_to_all(parts, "ctx", 0, 0, tiled=True, axis_index_groups=SAME_CORE)


def chip_sum(own, other):
    return (own.astype(F32) + swap(other).astype(F32)).astype(BF16)


def after(value, *earlier):
    return lax.optimization_barrier((value, *earlier))[0]


def per_device(hidden_in, query, key, value, out_weight, grad_out, span_map, owner_map):
    ids = jnp.stack([lax.axis_index("ctx"), lax.axis_index("head")]).astype(jnp.int32)
    grad = lax.all_gather(grad_out, "head", axis=1, tiled=True)
    kv_pieces = gather_over_ctx(jnp.concatenate([key, value], axis=1))
    query_other = swap(query)
    attn, lse = forward(ids, span_map, after(query, query_other), kv_pieces)
    hidden = lax.all_gather(after(hidden_in, attn), "head", axis=1, tiled=True)
    d_attn = nt(after(grad, attn), out_weight).astype(BF16)
    attn_other = swap(attn)
    sides = (query, query_other, d_attn, swap(d_attn), attn, attn_other, lse, swap(lse))
    dkv = backward(ids, span_map, sides, kv_pieces[:8])
    attn_late = after(attn, dkv)
    dkv = exchange(dkv).reshape(CHIPS, TOKENS, 2 * HEAD_SIZE)
    out_parts = out_gradient(ids, owner_map, attn_late, attn_other, grad, swap(grad))
    out_parts = exchange(after(out_parts, dkv))
    kv_total = chip_sum(*kv_gradient(ids, owner_map, dkv, hidden))
    kv_total = exchange(after(kv_total, out_parts))
    kv_total = jnp.sum(kv_total.astype(F32), axis=0)
    out_total = jnp.sum(out_parts.astype(F32), axis=0)
    return kv_total[:HEAD_SIZE].T, kv_total[HEAD_SIZE:].T, out_total


def solution(mesh):
    return jax.shard_map(
        per_device,
        mesh=mesh,
        in_specs=(
            P("ctx", "head"),
            P("ctx", "head"),
            P("ctx", "head"),
            P("ctx", "head"),
            P("head", None),
            P("ctx", "head"),
            P(),
            P(),
        ),
        out_specs=(P("ctx", "head"), P("ctx", "head"), P("head", "ctx")),
        check_vma=False,
    )
```

```python
import jax
import jax.numpy as jnp
from jax import lax
from jax.experimental import pallas as pl
from jax.experimental.pallas import tpu as pltpu
from jax.sharding import PartitionSpec as P

HEAD_SIZE = 128
GROUP = 4
SPAN = 192
SLOTS = 32
N_CTX = 16
CHIPS = 8
TOKENS = 384
KEY_BLOCK = 384
KEY_BLOCKS = 16
OUT_FLOPS = 8_000_000_000
OWN_BLOCKS = 8
WIDE = 3
ROWS = GROUP * SPAN
FEATURES = 256
HEAD_COLUMNS = 512
SCALE = HEAD_SIZE ** (-0.5)
EXP2_SCALE = SCALE * 1.4426950408889634
F32 = jnp.float32
BF16 = jnp.bfloat16
VMEM_BYTES = 58 * 1024 * 1024


def ctx_move(value, dx, dz, dc):
    pairs = []
    for i in range(N_CTX):
        x, z, c = i // 8, (i // 2) % 4, i % 2
        pairs.append((i, ((x ^ dx) * 4 + (z + dz) % 4) * 2 + (c ^ dc)))
    return lax.ppermute(value, "ctx", pairs)


STEPS = ((0, 0), (1, 0), (0, 3), (0, 1), (1, 3), (1, 1), (0, 2), (1, 2))


def gather_over_ctx(own):
    across = ctx_move(own, 1, 0, 0)
    up0 = ctx_move(own, 0, 1, 0)
    down0 = ctx_move(own, 0, 3, 0)
    up1 = ctx_move(across, 0, 1, 0)
    down1 = ctx_move(across, 0, 3, 0)
    far0 = ctx_move(up0, 0, 1, 0)
    far1 = ctx_move(down1, 0, 3, 0)
    mine = [own, across, up0, down0, up1, down1, far0, far1]
    return mine + [swap(piece) for piece in mine]


def swap(value):
    return ctx_move(value, 0, 0, 1)


def head_flip(value):
    return lax.ppermute(value, "head", [(i, i ^ 4) for i in range(8)])


SAME_X = [[0, 1, 2, 3], [4, 5, 6, 7]]


def source_of(ids, step, other_core):
    x, z, c = ids[0] // 8, (ids[0] // 2) % 4, ids[0] % 2
    dx, dz = STEPS[step]
    return ((x ^ dx) * 4 + (z + dz) % 4) * 2 + (c ^ other_core)


def nt(a, b):
    return lax.dot_general(a, b, (((1,), (1,)), ((), ())), preferred_element_type=F32)


def nn(a, b):
    return lax.dot_general(a, b, (((1,), (0,)), ((), ())), preferred_element_type=F32)


def key_rows(b):
    return pl.ds(pl.multiple_of(b * KEY_BLOCK, KEY_BLOCK), KEY_BLOCK)


def span_rows(n):
    return pl.ds(pl.multiple_of(n * SPAN, SPAN), SPAN)


def heads_down(value, half):
    rows = value[half * SPAN : (half + 1) * SPAN]
    return jnp.concatenate(
        [rows[:, h * HEAD_SIZE : (h + 1) * HEAD_SIZE] for h in range(GROUP)], axis=0
    )


def row_in_span(shape, dim):
    row = lax.broadcasted_iota(jnp.int32, shape, dim)
    within = row
    for h in range(1, GROUP):
        within = within - jnp.where(row >= h * SPAN, SPAN, 0)
    return within


def forward_kernel(ids, spans, q_ref, *rest):
    kv_refs, (attn_ref, lse_ref, ks, vs, qs, acc, tops, sums) = rest[:16], rest[16:]
    for piece in range(16):
        source = source_of(ids, piece % 8, piece // 8)
        for half in range(2):
            at, rows = span_rows(spans[source, half]), pl.ds(half * SPAN, SPAN)
            ks[at, :] = kv_refs[piece][rows, :HEAD_SIZE]
            vs[at, :] = kv_refs[piece][rows, HEAD_SIZE:]
    for half in range(2):
        qs[half] = heads_down(q_ref[...], half)

    for half in range(2):
        span = spans[ids[0], half]
        last = span // 2

        def step(b, masked):
            s = nt(qs[half], ks[key_rows(b), :])
            if masked:
                seen = span * SPAN + row_in_span((ROWS, 1), 0) - b * KEY_BLOCK
                s = jnp.where(lax.broadcasted_iota(jnp.int32, s.shape, 1) > seen, -1e30, s)
            old = tops[...]
            new = jnp.maximum(old, jnp.max(s, axis=1, keepdims=True))
            shrink = jnp.exp2((old - new) * EXP2_SCALE)
            tops[...] = new
            total, low = 0.0, []
            for k in range(0, KEY_BLOCK, HEAD_SIZE):
                p = jnp.exp2((s[:, k : k + HEAD_SIZE] - new) * EXP2_SCALE)
                total = total + p
                low.append(p.astype(BF16))
            sums[...] = sums[...] * shrink + total
            acc[...] = acc[...] * shrink + nn(jnp.concatenate(low, axis=1), vs[key_rows(b), :])

        tops[...] = jnp.full(tops.shape, -1e30, F32)
        sums[...] = jnp.zeros(sums.shape, F32)
        acc[...] = jnp.zeros(acc.shape, F32)

        @pl.loop(0, last)
        def _(b):
            step(b, False)

        step(last, True)
        total = jnp.sum(sums[...], axis=1, keepdims=True)
        attn = (acc[...] * (1.0 / total)).astype(BF16)
        for h in range(GROUP):
            attn_ref[pl.ds(half * SPAN, SPAN), pl.ds(h * HEAD_SIZE, HEAD_SIZE)] = attn[
                h * SPAN : (h + 1) * SPAN
            ]
        lse_ref[half] = (tops[...] * EXP2_SCALE + jnp.log2(total)).T[:8]


def smem():
    return pl.BlockSpec(memory_space=pltpu.SMEM)


def vmem():
    return pl.BlockSpec(memory_space=pltpu.VMEM)


def call(kernel, inputs, outputs, scratch, flops, name):
    return pl.pallas_call(
        kernel,
        out_shape=outputs,
        in_specs=[smem(), smem()] + [vmem()] * (len(inputs) - 2),
        out_specs=(vmem(),) * len(outputs),
        scratch_shapes=scratch,
        compiler_params=pltpu.CompilerParams(vmem_limit_bytes=VMEM_BYTES),
        cost_estimate=pl.CostEstimate(flops=flops, bytes_accessed=1024, transcendentals=0),
        name=name,
    )(*inputs)


def forward(ids, span_map, query, kv_pieces):
    keys = pltpu.VMEM((KEY_BLOCKS * KEY_BLOCK, HEAD_SIZE), BF16)
    rows = pltpu.VMEM((ROWS, HEAD_SIZE), F32)
    return call(
        forward_kernel,
        (ids, span_map, query, *kv_pieces),
        (
            jax.ShapeDtypeStruct(query.shape, BF16),
            jax.ShapeDtypeStruct((2, 8, ROWS), F32),
        ),
        [keys, keys, pltpu.VMEM((2, ROWS, HEAD_SIZE), BF16), rows, rows, rows],
        1_000_000,
        "forward",
    )


def backward_kernel(ids, spans, *rest):
    (q_own, q_other, do_own, do_other, attn_own, attn_other, lse_own, lse_other), rest = (
        rest[:8],
        rest[8:],
    )
    kv_refs, (part_ref, ks, vs, qs, dos, lse, delta, acc_k, acc_v, slot, rank, seen, order) = (
        rest[:8],
        rest[8:],
    )
    core = ids[0] % 2
    for s in range(SLOTS):
        slot[s] = 0
    for chip in range(CHIPS):
        for half in range(2):
            slot[spans[chip * 2 + core, half]] = chip * 2 + half + 1
    count = jnp.int32(0)
    for s in range(SLOTS):
        order[count] = s
        rank[s] = count
        count = count + jnp.minimum(slot[s], 1)
        seen[s] = count

    for piece in range(8):
        source = source_of(ids, piece, 0)
        for half in range(2):
            at, rows = span_rows(rank[spans[source, half]]), pl.ds(half * SPAN, SPAN)
            ks[at, :] = kv_refs[piece][rows, :HEAD_SIZE]
            vs[at, :] = kv_refs[piece][rows, HEAD_SIZE:]
    sides = ((q_own, do_own, attn_own, lse_own), (q_other, do_other, attn_other, lse_other))
    for side, (q_ref, do_ref, attn_ref, lse_ref) in enumerate(sides):
        product = do_ref[...].astype(F32) * attn_ref[...].astype(F32)
        for half in range(2):
            qs[side * 2 + half] = heads_down(q_ref[...], half)
            dos[side * 2 + half] = heads_down(do_ref[...], half)
            lse[side * 2 + half] = lse_ref[half, :1]
            delta[side * 2 + half] = jnp.sum(heads_down(product, half).T, axis=0, keepdims=True)

    acc_k[...] = jnp.zeros(acc_k.shape, F32)
    acc_v[...] = jnp.zeros(acc_v.shape, F32)

    def tile(first, count, group, span, masked):
        rows = pl.ds(pl.multiple_of(first, KEY_BLOCK), count)
        s = nt(ks[rows, :], qs[group])
        if masked:
            b = first // KEY_BLOCK
            row = lax.broadcasted_iota(jnp.int32, (count, 1), 0)
            at = jnp.where(row < SPAN, order[b * 2] * SPAN, (order[b * 2 + 1] - 1) * SPAN) + row
            s = jnp.where(at > span * SPAN + row_in_span((1, ROWS), 1), -1e30, s)
        p = jnp.exp2(s * EXP2_SCALE - lse[group])
        d_p = nt(vs[rows, :], dos[group])
        d_s = (p * (d_p - delta[group])).astype(BF16)
        acc_k[rows, :] += nn(d_s, qs[group])
        acc_v[rows, :] += nn(p.astype(BF16), dos[group])

    @pl.loop(0, 4)
    def _(group):
        span = spans[ids[0] ^ (group // 2), group % 2]
        last = (seen[span] + 1) // 2 - 1
        wide = jnp.maximum(last, 0) // WIDE

        @pl.loop(0, wide)
        def _(n):
            tile(n * WIDE * KEY_BLOCK, WIDE * KEY_BLOCK, group, span, False)

        @pl.loop(wide * WIDE, last)
        def _(b):
            tile(b * KEY_BLOCK, KEY_BLOCK, group, span, False)

        @pl.when(last >= 0)
        def _():
            tile(last * KEY_BLOCK, KEY_BLOCK, group, span, True)

    for n in range(2 * CHIPS):
        at = slot[order[n]] - 1
        rows = pl.ds(n * SPAN, SPAN)
        part_ref[at, :, :HEAD_SIZE] = (acc_k[rows, :] * SCALE).astype(BF16)
        part_ref[at, :, HEAD_SIZE:] = acc_v[rows, :].astype(BF16)


def backward(ids, span_map, sides, kv_pieces):
    keys = pltpu.VMEM((OWN_BLOCKS * KEY_BLOCK, HEAD_SIZE), BF16)
    rows = pltpu.VMEM((4, ROWS, HEAD_SIZE), BF16)
    stats = pltpu.VMEM((4, 1, ROWS), F32)
    sums = pltpu.VMEM((OWN_BLOCKS * KEY_BLOCK, HEAD_SIZE), F32)
    table = pltpu.SMEM((SLOTS,), jnp.int32)
    (part,) = call(
        backward_kernel,
        (ids, span_map, *sides, *kv_pieces),
        (jax.ShapeDtypeStruct((2 * CHIPS, SPAN, 2 * HEAD_SIZE), BF16),),
        [keys, keys, rows, rows, stats, stats, sums, sums, table, table, table, table],
        1_000_000,
        "backward",
    )
    return part


def blocks_by_owner(owners, n, found):
    for b in range(N_CTX):
        found[owners[n, b]] = b


def paired_block(ids, b):
    x, y, half = b // 8, (b // 2) % 4, b % 2
    return y * 4 + (x ^ (ids[1] // 4)) * 2 + half


def feature_block(ref, b):
    return ref[:, pl.ds(pl.multiple_of(b * FEATURES, FEATURES), FEATURES)]


def out_kernel(ids, owners, attn_own, attn_other, grad_own, grad_other, out_ref, found):
    core = ids[0] % 2
    blocks_by_owner(owners, 2, found)
    attn_t = [ref[...].astype(F32).T.astype(BF16) for ref in (attn_own, attn_other)]
    for chip in range(CHIPS):
        b = found[chip * 2 + core]
        block = nn(attn_t[0], feature_block(grad_own, b)) + nn(
            attn_t[1], feature_block(grad_other, b)
        )
        out_ref[chip] = block.astype(BF16)


def out_gradient(ids, owner_map, attn, attn_other, grad, grad_other):
    part = jax.ShapeDtypeStruct((CHIPS, HEAD_COLUMNS, FEATURES), BF16)
    (parts,) = call(
        out_kernel,
        (ids, owner_map, attn, attn_other, grad, grad_other),
        (part,),
        [pltpu.SMEM((N_CTX,), jnp.int32)],
        OUT_FLOPS,
        "out_gradient",
    )
    return parts


def kv_kernel(ids, owners, parts_ref, hidden_ref, own_ref, other_ref, found_k, found_v):
    core = ids[0] % 2
    blocks_by_owner(owners, 0, found_k)
    blocks_by_owner(owners, 1, found_v)
    total = jnp.sum(parts_ref[...].astype(F32), axis=0)
    both = []
    for n in range(2):
        t = total[:, n * HEAD_SIZE : (n + 1) * HEAD_SIZE].T
        high = t.astype(BF16)
        both.append(jnp.concatenate([high, (t - high.astype(F32)).astype(BF16)], axis=0))
    for out_ref, at in ((other_ref, 1 - core), (own_ref, core)):
        for chip in range(CHIPS):
            for n, found in enumerate((found_k, found_v)):
                block = nn(both[n], feature_block(hidden_ref, paired_block(ids, found[chip * 2 + at])))
                out_ref[chip, n * HEAD_SIZE : (n + 1) * HEAD_SIZE, :] = (
                    block[:HEAD_SIZE] + block[HEAD_SIZE:]
                ).astype(BF16)


def kv_gradient(ids, owner_map, parts, hidden):
    part = jax.ShapeDtypeStruct((CHIPS, 2 * HEAD_SIZE, FEATURES), BF16)
    found = pltpu.SMEM((N_CTX,), jnp.int32)
    return call(
        kv_kernel,
        (ids, owner_map, parts, hidden),
        (part, part),
        [found, found],
        1_000_000,
        "kv_gradient",
    )


SAME_CORE = [[c + 2 * chip for chip in range(CHIPS)] for c in range(2)]


def exchange(parts):
    return lax.all_to_all(parts, "ctx", 0, 0, tiled=True, axis_index_groups=SAME_CORE)


def chip_sum(own, other):
    return (own.astype(F32) + swap(other).astype(F32)).astype(BF16)


def after(value, *earlier):
    return lax.optimization_barrier((value, *earlier))[0]


def per_device(hidden_in, query, key, value, out_weight, grad_out, span_map, owner_map):
    ids = jnp.stack([lax.axis_index("ctx"), lax.axis_index("head")]).astype(jnp.int32)
    grad = lax.all_gather(grad_out, "head", axis=1, tiled=True)
    kv_pieces = gather_over_ctx(jnp.concatenate([key, value], axis=1))
    query_other = swap(query)
    attn, lse = forward(ids, span_map, after(query, query_other), kv_pieces)
    hidden_other = head_flip(after(hidden_in, attn))
    d_attn = nt(after(grad, attn), out_weight).astype(BF16)
    attn_other = swap(attn)
    out_parts = out_gradient(
        ids, owner_map, after(attn, d_attn), attn_other, grad, swap(after(grad, attn))
    )
    hidden_pair = jnp.concatenate([hidden_in, after(hidden_other, out_parts)], axis=1)
    hidden = lax.all_gather(hidden_pair, "head", axis=1, tiled=True, axis_index_groups=SAME_X)
    query_late = after(query, out_parts, hidden_pair)
    out_parts = exchange(out_parts)
    sides = (query_late, query_other, d_attn, swap(d_attn), attn, attn_other, lse, swap(lse))
    dkv = backward(ids, span_map, sides, kv_pieces[:8])
    dkv = exchange(after(dkv, out_parts)).reshape(CHIPS, TOKENS, 2 * HEAD_SIZE)
    kv_total = exchange(chip_sum(*kv_gradient(ids, owner_map, dkv, hidden)))
    kv_total = jnp.sum(kv_total.astype(F32), axis=0)
    out_total = jnp.sum(out_parts.astype(F32), axis=0)
    return kv_total[:HEAD_SIZE].T, kv_total[HEAD_SIZE:].T, out_total


def solution(mesh):
    return jax.shard_map(
        per_device,
        mesh=mesh,
        in_specs=(
            P("ctx", "head"),
            P("ctx", "head"),
            P("ctx", "head"),
            P("ctx", "head"),
            P("head", None),
            P("ctx", "head"),
            P(),
            P(),
        ),
        out_specs=(P("ctx", "head"), P("ctx", "head"), P("head", "ctx")),
        check_vma=False,
    )
```

```python
import jax
import jax.numpy as jnp
from jax import lax
from jax.experimental import pallas as pl
from jax.experimental.pallas import tpu as pltpu
from jax.sharding import PartitionSpec as P

HEAD_SIZE = 128
GROUP = 4
SPAN = 192
SLOTS = 32
N_CTX = 16
CHIPS = 8
TOKENS = 384
KEY_BLOCK = 384
KEY_BLOCKS = 16
OUT_FLOPS = 8_000_000_000
OWN_BLOCKS = 8
WIDE = 3
ROWS = GROUP * SPAN
FEATURES = 256
HEAD_COLUMNS = 512
SCALE = HEAD_SIZE ** (-0.5)
EXP2_SCALE = SCALE * 1.4426950408889634
F32 = jnp.float32
BF16 = jnp.bfloat16
VMEM_BYTES = 58 * 1024 * 1024
SMALL_VMEM_BYTES = 20 * 1024 * 1024


def ctx_move(value, dx, dz, dc):
    pairs = []
    for i in range(N_CTX):
        x, z, c = i // 8, (i // 2) % 4, i % 2
        pairs.append((i, ((x ^ dx) * 4 + (z + dz) % 4) * 2 + (c ^ dc)))
    return lax.ppermute(value, "ctx", pairs)


STEPS = ((0, 0), (1, 0), (0, 3), (0, 1), (1, 3), (1, 1), (0, 2), (1, 2))


def gather_over_ctx(own):
    across = ctx_move(own, 1, 0, 0)
    up0 = ctx_move(own, 0, 1, 0)
    down0 = ctx_move(own, 0, 3, 0)
    up1 = ctx_move(across, 0, 1, 0)
    down1 = ctx_move(across, 0, 3, 0)
    far0 = ctx_move(up0, 0, 1, 0)
    far1 = ctx_move(down1, 0, 3, 0)
    mine = [own, across, up0, down0, up1, down1, far0, far1]
    return mine + [swap(piece) for piece in mine]


def swap(value):
    return ctx_move(value, 0, 0, 1)


def head_flip(value):
    return lax.ppermute(value, "head", [(i, i ^ 4) for i in range(8)])


SAME_X = [[0, 1, 2, 3], [4, 5, 6, 7]]


def source_of(ids, step, other_core):
    x, z, c = ids[0] // 8, (ids[0] // 2) % 4, ids[0] % 2
    dx, dz = STEPS[step]
    return ((x ^ dx) * 4 + (z + dz) % 4) * 2 + (c ^ other_core)


def nt(a, b):
    return lax.dot_general(a, b, (((1,), (1,)), ((), ())), preferred_element_type=F32)


def nn(a, b):
    return lax.dot_general(a, b, (((1,), (0,)), ((), ())), preferred_element_type=F32)


def key_rows(b):
    return pl.ds(pl.multiple_of(b * KEY_BLOCK, KEY_BLOCK), KEY_BLOCK)


def span_rows(n):
    return pl.ds(pl.multiple_of(n * SPAN, SPAN), SPAN)


def heads_down(value, half):
    rows = value[half * SPAN : (half + 1) * SPAN]
    return jnp.concatenate(
        [rows[:, h * HEAD_SIZE : (h + 1) * HEAD_SIZE] for h in range(GROUP)], axis=0
    )


def row_in_span(shape, dim):
    row = lax.broadcasted_iota(jnp.int32, shape, dim)
    within = row
    for h in range(1, GROUP):
        within = within - jnp.where(row >= h * SPAN, SPAN, 0)
    return within


def forward_kernel(ids, spans, q_ref, *rest):
    kv_refs, (attn_ref, lse_ref, ks, vs, qs, acc, tops, sums) = rest[:16], rest[16:]
    for piece in range(16):
        source = source_of(ids, piece % 8, piece // 8)
        for half in range(2):
            at, rows = span_rows(spans[source, half]), pl.ds(half * SPAN, SPAN)
            ks[at, :] = kv_refs[piece][rows, :HEAD_SIZE]
            vs[at, :] = kv_refs[piece][rows, HEAD_SIZE:]
    for half in range(2):
        qs[half] = heads_down(q_ref[...], half)

    for half in range(2):
        span = spans[ids[0], half]
        last = span // 2

        def step(b, masked):
            s = nt(qs[half], ks[key_rows(b), :])
            if masked:
                seen = span * SPAN + row_in_span((ROWS, 1), 0) - b * KEY_BLOCK
                s = jnp.where(lax.broadcasted_iota(jnp.int32, s.shape, 1) > seen, -1e30, s)
            old = tops[...]
            new = jnp.maximum(old, jnp.max(s, axis=1, keepdims=True))
            shrink = jnp.exp2((old - new) * EXP2_SCALE)
            tops[...] = new
            total, low = 0.0, []
            for k in range(0, KEY_BLOCK, HEAD_SIZE):
                p = jnp.exp2((s[:, k : k + HEAD_SIZE] - new) * EXP2_SCALE)
                total = total + p
                low.append(p.astype(BF16))
            sums[...] = sums[...] * shrink + total
            acc[...] = acc[...] * shrink + nn(jnp.concatenate(low, axis=1), vs[key_rows(b), :])

        tops[...] = jnp.full(tops.shape, -1e30, F32)
        sums[...] = jnp.zeros(sums.shape, F32)
        acc[...] = jnp.zeros(acc.shape, F32)

        @pl.loop(0, last)
        def _(b):
            step(b, False)

        step(last, True)
        total = jnp.sum(sums[...], axis=1, keepdims=True)
        attn = (acc[...] * (1.0 / total)).astype(BF16)
        for h in range(GROUP):
            attn_ref[pl.ds(half * SPAN, SPAN), pl.ds(h * HEAD_SIZE, HEAD_SIZE)] = attn[
                h * SPAN : (h + 1) * SPAN
            ]
        lse_ref[half] = (tops[...] * EXP2_SCALE + jnp.log2(total)).T[:8]


def smem():
    return pl.BlockSpec(memory_space=pltpu.SMEM)


def vmem():
    return pl.BlockSpec(memory_space=pltpu.VMEM)


def call(kernel, inputs, outputs, scratch, flops, name, vmem_bytes=VMEM_BYTES):
    return pl.pallas_call(
        kernel,
        out_shape=outputs,
        in_specs=[smem(), smem()] + [vmem()] * (len(inputs) - 2),
        out_specs=(vmem(),) * len(outputs),
        scratch_shapes=scratch,
        compiler_params=pltpu.CompilerParams(vmem_limit_bytes=vmem_bytes),
        cost_estimate=pl.CostEstimate(flops=flops, bytes_accessed=1024, transcendentals=0),
        name=name,
    )(*inputs)


def forward(ids, span_map, query, kv_pieces):
    keys = pltpu.VMEM((KEY_BLOCKS * KEY_BLOCK, HEAD_SIZE), BF16)
    rows = pltpu.VMEM((ROWS, HEAD_SIZE), F32)
    return call(
        forward_kernel,
        (ids, span_map, query, *kv_pieces),
        (
            jax.ShapeDtypeStruct(query.shape, BF16),
            jax.ShapeDtypeStruct((2, 8, ROWS), F32),
        ),
        [keys, keys, pltpu.VMEM((2, ROWS, HEAD_SIZE), BF16), rows, rows, rows],
        1_000_000,
        "forward",
    )


def backward_kernel(ids, spans, *rest):
    (q_own, q_other, do_own, do_other, attn_own, attn_other, lse_own, lse_other), rest = (
        rest[:8],
        rest[8:],
    )
    kv_refs, (part_ref, ks, vs, qs, dos, lse, delta, acc_k, acc_v, slot, rank, seen, order) = (
        rest[:8],
        rest[8:],
    )
    core = ids[0] % 2
    for s in range(SLOTS):
        slot[s] = 0
    for chip in range(CHIPS):
        for half in range(2):
            slot[spans[chip * 2 + core, half]] = chip * 2 + half + 1
    count = jnp.int32(0)
    for s in range(SLOTS):
        order[count] = s
        rank[s] = count
        count = count + jnp.minimum(slot[s], 1)
        seen[s] = count

    for piece in range(8):
        source = source_of(ids, piece, 0)
        for half in range(2):
            at, rows = span_rows(rank[spans[source, half]]), pl.ds(half * SPAN, SPAN)
            ks[at, :] = kv_refs[piece][rows, :HEAD_SIZE]
            vs[at, :] = kv_refs[piece][rows, HEAD_SIZE:]
    sides = ((q_own, do_own, attn_own, lse_own), (q_other, do_other, attn_other, lse_other))
    for side, (q_ref, do_ref, attn_ref, lse_ref) in enumerate(sides):
        product = do_ref[...].astype(F32) * attn_ref[...].astype(F32)
        for half in range(2):
            qs[side * 2 + half] = heads_down(q_ref[...], half)
            dos[side * 2 + half] = heads_down(do_ref[...], half)
            lse[side * 2 + half] = lse_ref[half, :1]
            delta[side * 2 + half] = jnp.sum(heads_down(product, half).T, axis=0, keepdims=True)

    acc_k[...] = jnp.zeros(acc_k.shape, F32)
    acc_v[...] = jnp.zeros(acc_v.shape, F32)

    def tile(first, count, group, span, masked):
        rows = pl.ds(pl.multiple_of(first, KEY_BLOCK), count)
        s = nt(ks[rows, :], qs[group])
        if masked:
            b = first // KEY_BLOCK
            row = lax.broadcasted_iota(jnp.int32, (count, 1), 0)
            at = jnp.where(row < SPAN, order[b * 2] * SPAN, (order[b * 2 + 1] - 1) * SPAN) + row
            s = jnp.where(at > span * SPAN + row_in_span((1, ROWS), 1), -1e30, s)
        p = jnp.exp2(s * EXP2_SCALE - lse[group])
        d_p = nt(vs[rows, :], dos[group])
        d_s = (p * (d_p - delta[group])).astype(BF16)
        acc_k[rows, :] += nn(d_s, qs[group])
        acc_v[rows, :] += nn(p.astype(BF16), dos[group])

    @pl.loop(0, 4)
    def _(group):
        span = spans[ids[0] ^ (group // 2), group % 2]
        last = (seen[span] + 1) // 2 - 1
        wide = jnp.maximum(last, 0) // WIDE

        @pl.loop(0, wide)
        def _(n):
            tile(n * WIDE * KEY_BLOCK, WIDE * KEY_BLOCK, group, span, False)

        @pl.loop(wide * WIDE, last)
        def _(b):
            tile(b * KEY_BLOCK, KEY_BLOCK, group, span, False)

        @pl.when(last >= 0)
        def _():
            tile(last * KEY_BLOCK, KEY_BLOCK, group, span, True)

    for n in range(2 * CHIPS):
        at = slot[order[n]] - 1
        rows = pl.ds(n * SPAN, SPAN)
        part_ref[at, :, :HEAD_SIZE] = (acc_k[rows, :] * SCALE).astype(BF16)
        part_ref[at, :, HEAD_SIZE:] = acc_v[rows, :].astype(BF16)


def backward(ids, span_map, sides, kv_pieces):
    keys = pltpu.VMEM((OWN_BLOCKS * KEY_BLOCK, HEAD_SIZE), BF16)
    rows = pltpu.VMEM((4, ROWS, HEAD_SIZE), BF16)
    stats = pltpu.VMEM((4, 1, ROWS), F32)
    sums = pltpu.VMEM((OWN_BLOCKS * KEY_BLOCK, HEAD_SIZE), F32)
    table = pltpu.SMEM((SLOTS,), jnp.int32)
    (part,) = call(
        backward_kernel,
        (ids, span_map, *sides, *kv_pieces),
        (jax.ShapeDtypeStruct((2 * CHIPS, SPAN, 2 * HEAD_SIZE), BF16),),
        [keys, keys, rows, rows, stats, stats, sums, sums, table, table, table, table],
        1_000_000,
        "backward",
    )
    return part


def blocks_by_owner(owners, n, found):
    for b in range(N_CTX):
        found[owners[n, b]] = b


def paired_block(ids, b):
    x, y, half = b // 8, (b // 2) % 4, b % 2
    return y * 4 + (x ^ (ids[1] // 4)) * 2 + half


def feature_block(ref, b):
    return ref[:, pl.ds(pl.multiple_of(b * FEATURES, FEATURES), FEATURES)]


def out_kernel(ids, owners, attn_own, attn_other, grad_own, grad_other, out_ref, found):
    core = ids[0] % 2
    blocks_by_owner(owners, 2, found)
    attn_t = [ref[...].astype(F32).T.astype(BF16) for ref in (attn_own, attn_other)]
    for chip in range(CHIPS):
        b = found[chip * 2 + core]
        block = nn(attn_t[0], feature_block(grad_own, b)) + nn(
            attn_t[1], feature_block(grad_other, b)
        )
        out_ref[chip] = block.astype(BF16)


def out_gradient(ids, owner_map, attn, attn_other, grad, grad_other):
    part = jax.ShapeDtypeStruct((CHIPS, HEAD_COLUMNS, FEATURES), BF16)
    (parts,) = call(
        out_kernel,
        (ids, owner_map, attn, attn_other, grad, grad_other),
        (part,),
        [pltpu.SMEM((N_CTX,), jnp.int32)],
        OUT_FLOPS,
        "out_gradient",
        SMALL_VMEM_BYTES,
    )
    return parts


def kv_kernel(ids, owners, parts_ref, hidden_ref, own_ref, other_ref, found_k, found_v):
    core = ids[0] % 2
    blocks_by_owner(owners, 0, found_k)
    blocks_by_owner(owners, 1, found_v)
    total = jnp.sum(parts_ref[...].astype(F32), axis=0)
    both = []
    for n in range(2):
        t = total[:, n * HEAD_SIZE : (n + 1) * HEAD_SIZE].T
        high = t.astype(BF16)
        both.append(jnp.concatenate([high, (t - high.astype(F32)).astype(BF16)], axis=0))
    for out_ref, at in ((other_ref, 1 - core), (own_ref, core)):
        for chip in range(CHIPS):
            for n, found in enumerate((found_k, found_v)):
                block = nn(both[n], feature_block(hidden_ref, paired_block(ids, found[chip * 2 + at])))
                out_ref[chip, n * HEAD_SIZE : (n + 1) * HEAD_SIZE, :] = (
                    block[:HEAD_SIZE] + block[HEAD_SIZE:]
                ).astype(BF16)


def kv_gradient(ids, owner_map, parts, hidden):
    part = jax.ShapeDtypeStruct((CHIPS, 2 * HEAD_SIZE, FEATURES), BF16)
    found = pltpu.SMEM((N_CTX,), jnp.int32)
    return call(
        kv_kernel,
        (ids, owner_map, parts, hidden),
        (part, part),
        [found, found],
        1_000_000,
        "kv_gradient",
        SMALL_VMEM_BYTES,
    )


SAME_CORE = [[c + 2 * chip for chip in range(CHIPS)] for c in range(2)]


def exchange(parts):
    return lax.all_to_all(parts, "ctx", 0, 0, tiled=True, axis_index_groups=SAME_CORE)


def chip_sum(own, other):
    return (own.astype(F32) + swap(other).astype(F32)).astype(BF16)


def after(value, *earlier):
    return lax.optimization_barrier((value, *earlier))[0]


def per_device(hidden_in, query, key, value, out_weight, grad_out, span_map, owner_map):
    ids = jnp.stack([lax.axis_index("ctx"), lax.axis_index("head")]).astype(jnp.int32)
    grad = lax.all_gather(grad_out, "head", axis=1, tiled=True)
    kv_pieces = gather_over_ctx(jnp.concatenate([key, value], axis=1))
    query_other = swap(query)
    attn, lse = forward(ids, span_map, after(query, query_other), kv_pieces)
    hidden_other = head_flip(after(hidden_in, attn))
    d_attn = nt(after(grad, attn), out_weight).astype(BF16)
    attn_other = swap(attn)
    out_parts = out_gradient(
        ids, owner_map, after(attn, d_attn), attn_other, grad, swap(after(grad, attn))
    )
    hidden_pair = jnp.concatenate([hidden_in, after(hidden_other, out_parts)], axis=1)
    hidden = lax.all_gather(hidden_pair, "head", axis=1, tiled=True, axis_index_groups=SAME_X)
    query_late = after(query, out_parts, hidden_pair)
    out_parts = exchange(out_parts)
    sides = (query_late, query_other, d_attn, swap(d_attn), attn, attn_other, lse, swap(lse))
    dkv = backward(ids, span_map, sides, kv_pieces[:8])
    dkv = exchange(after(dkv, out_parts)).reshape(CHIPS, TOKENS, 2 * HEAD_SIZE)
    kv_total = exchange(chip_sum(*kv_gradient(ids, owner_map, dkv, hidden)))
    kv_total = jnp.sum(kv_total.astype(F32), axis=0)
    out_total = jnp.sum(out_parts.astype(F32), axis=0)
    return kv_total[:HEAD_SIZE].T, kv_total[HEAD_SIZE:].T, out_total


def solution(mesh):
    return jax.shard_map(
        per_device,
        mesh=mesh,
        in_specs=(
            P("ctx", "head"),
            P("ctx", "head"),
            P("ctx", "head"),
            P("ctx", "head"),
            P("head", None),
            P("ctx", "head"),
            P(),
            P(),
        ),
        out_specs=(P("ctx", "head"), P("ctx", "head"), P("head", "ctx")),
        check_vma=False,
    )
```
